128 devices in a mesh: outer: 16 (over x_hi, z, core), inner: 8 (over y, x_lo).
Axes of the slice: x: 4 (x_hi: 2, x_lo: 2; x = x_hi * 2 + x_lo), y: 4, z: 4, core: 2. Of those that a mesh axis runs over, the one named last changes fastest.
Arguments:
- queries: bfloat16 [16384, 2048], P(('outer', 'inner')), may hold values from -80 to 80
- key_vals: bfloat16 [16384, 512], P(('outer', 'inner')), may hold values from -6 to 6
- key_block_scale: bfloat16 [16384, 4], P(('outer', 'inner')), may hold values from 0.5 to 2
- stored_value_entries: bfloat16 [16384, 512], P(('outer', 'inner')), may hold values from -6 to 6
- value_block_scale: bfloat16 [16384, 4], P(('outer', 'inner')), may hold values from 0.5 to 2
- span_pos: int32 [256], P(('outer', 'inner')), may hold values from 0 to 255, each once
- page_of_slot: int32 [256], P(('outer', 'inner')), may hold values from 0 to 255, each once
Outputs:
- attended: bfloat16 [16384, 2048], P(('outer', 'inner'))
- slot_page_keys: bfloat16 [256, 64, 512], P(('outer', 'inner'))
- slot_page_values: bfloat16 [256, 64, 512], P(('outer', 'inner'))
The draws below stay inside these ranges and needn't reach their ends.
Inputs may be any that keep to these rules, and one draw needn't show every extreme that they name: `span_pos`: each span position occurs exactly once. `page_of_slot`: each page occurs exactly once.
All inputs are finite; a program needn't handle non-finite values.
Results may differ from the reference program's by a relative error of at most 0.0077.
Values may be sent and summed in bfloat16 or wider, within the bound.
No kernel may reach another device: no remote copies, remote signals or barrier semaphores. Data moves between devices by JAX's collectives and lax.ppermute only.
A program may use at most 384 MiB of HBM per device.

```python
import math
import jax
import jax.numpy as jnp
from jax import lax

LOCAL_QUERY_HEADS = 16
LOCAL_KEY_HEADS = 4
HEAD_DIMENSION = 128
SPAN_TOKENS = 64
SPAN_COUNT = 256
DOCUMENT_TOKENS = 16384


def shared_base(key):
    return jnp.clip(jax.random.normal(key, (DOCUMENT_TOKENS, LOCAL_KEY_HEADS * HEAD_DIMENSION), jnp.float32), -6.0, 6.0)


def draw_key_vals(key, part):
    base_offset = shared_base(key)
    return base_offset.astype(jnp.bfloat16)


def draw_queries(key, part):
    key = jax.random.fold_in(key, 5)
    noise = jnp.clip(jax.random.normal(key, (DOCUMENT_TOKENS, LOCAL_QUERY_HEADS * HEAD_DIMENSION), jnp.float32), -6.0, 6.0)
    return noise.astype(jnp.bfloat16)


def level_of(rng, extent, pieces, smallest, top_value):
    gain = 1.0
    for dim, blocks in pieces:
        heights = jax.random.uniform(jax.random.fold_in(jax.random.fold_in(rng, 6), dim), (blocks,), jnp.float32, smallest / len(pieces), top_value / len(pieces))
        gain = gain * jnp.repeat(jnp.exp(heights), extent[dim] // blocks).reshape((-1,) + (1,) * (len(extent) - 1 - dim))
    return gain


def bell_draw(rng, dims, deviation, reach, pieces=(), kind=jnp.bfloat16):
    array = jax.random.normal(rng, dims, jnp.float32) * deviation
    if len(pieces) > 0:
        array = level_of(rng, dims, pieces, -0.22, 0.18) * array
    return jnp.clip(array, min=-reach, max=reach).astype(kind)


def setup_inputs(seed: int = 0) -> dict:
    seeds = jax.random.split(jax.random.key(seed), 8)
    return {
        "queries": draw_queries(jax.random.fold_in(seeds[7], 71), 0),
        "key_vals": draw_key_vals(jax.random.fold_in(seeds[7], 71), 0),
        "key_block_scale": jnp.clip(jnp.exp(math.log(2.0) - 1.3862944 * jax.random.uniform(seeds[2], (DOCUMENT_TOKENS, LOCAL_KEY_HEADS), jnp.float32) ** level_of(seeds[2], (DOCUMENT_TOKENS, LOCAL_KEY_HEADS), ((0, 128),), -0.2, 0.2)), 0.5, 2.0).astype(jnp.bfloat16),
        "stored_value_entries": bell_draw(seeds[3], (DOCUMENT_TOKENS, LOCAL_KEY_HEADS * HEAD_DIMENSION), 1.0, 6.0, ((0, 128),)),
        "value_block_scale": jnp.clip(jnp.exp(math.log(2.0) - 1.3862944 * jax.random.uniform(seeds[4], (DOCUMENT_TOKENS, LOCAL_KEY_HEADS), jnp.float32) ** level_of(seeds[4], (DOCUMENT_TOKENS, LOCAL_KEY_HEADS), ((0, 128),), -0.2, 0.2)), 0.5, 2.0).astype(jnp.bfloat16),
        "span_pos": jax.random.permutation(seeds[5], SPAN_COUNT).astype(jnp.int32),
        "page_of_slot": jax.random.permutation(seeds[6], SPAN_COUNT).astype(jnp.int32),
    }


def dequantize(value_entries, scales):
    token_count = value_entries.shape[0]
    reshaped_array = value_entries.astype(jnp.float32).reshape(token_count, LOCAL_KEY_HEADS, HEAD_DIMENSION)
    return (reshaped_array * scales.astype(jnp.float32)[:, :, None]).astype(jnp.bfloat16)

def reference(queries, key_vals, key_block_scale, stored_value_entries, value_block_scale, span_pos, page_of_slot):
    query_groups = LOCAL_QUERY_HEADS // LOCAL_KEY_HEADS
    tok_index = jnp.arange(DOCUMENT_TOKENS, dtype=jnp.int32)
    position = (span_pos[tok_index // SPAN_TOKENS] * SPAN_TOKENS + tok_index % SPAN_TOKENS).astype(jnp.int32)
    key_rows = dequantize(key_vals, key_block_scale)
    value_rows = dequantize(stored_value_entries, value_block_scale)
    keys_wide = key_rows.astype(jnp.float32)
    values_wide = value_rows.astype(jnp.float32)
    block_length = math.gcd(512, DOCUMENT_TOKENS)
    query_block_list = queries.reshape(DOCUMENT_TOKENS // block_length, block_length, LOCAL_KEY_HEADS, query_groups, HEAD_DIMENSION)
    pos_blocks = position.reshape(DOCUMENT_TOKENS // block_length, block_length)
    factor = 1.0 / math.sqrt(HEAD_DIMENSION)

    def attend_block(inputs):
        q_block, p_block = inputs
        scores = jnp.einsum('qhgd,khd->hgqk', q_block.astype(jnp.float32), keys_wide) * factor
        visible = position[None, :] <= p_block[:, None]
        scores = jnp.where(visible, scores, -1e+30)
        row_max = lax.optimization_barrier(jnp.max(scores, axis=-1))
        weights = jnp.where(visible, jnp.exp(scores - row_max[..., None]), 0.0)
        totals = lax.optimization_barrier(jnp.sum(weights, axis=-1))
        rounded = weights.astype(jnp.bfloat16).astype(jnp.float32)
        outputs = jnp.einsum('hgqk,khd->hgqd', rounded, values_wide) / totals[..., None]
        outputs = jnp.transpose(outputs, (2, 0, 1, 3)).reshape(block_length, LOCAL_QUERY_HEADS * HEAD_DIMENSION)
        return outputs.astype(jnp.bfloat16)
    attended = lax.map(attend_block, (query_block_list, pos_blocks)).reshape(DOCUMENT_TOKENS, LOCAL_QUERY_HEADS * HEAD_DIMENSION)
    inverse = jnp.zeros((SPAN_COUNT,), jnp.int32).at[span_pos].set(jnp.arange(SPAN_COUNT, dtype=jnp.int32))
    source_array = inverse[page_of_slot]
    slot_page_keys = key_rows.reshape(SPAN_COUNT, SPAN_TOKENS, LOCAL_KEY_HEADS * HEAD_DIMENSION)[source_array]
    slot_page_values = value_rows.reshape(SPAN_COUNT, SPAN_TOKENS, LOCAL_KEY_HEADS * HEAD_DIMENSION)[source_array]
    return (attended, slot_page_keys, slot_page_values)
```

```python
import functools
import math

import jax
import jax.numpy as jnp
from jax import lax
from jax.experimental import pallas as pl
from jax.experimental.pallas import tpu as pltpu
from jax.sharding import Mesh
from jax.sharding import PartitionSpec as P

AXES = ("xh", "z", "c", "y", "xl")
X = ("xh", "xl")
BF16 = jnp.bfloat16
F32 = jnp.float32
SPAN = 64
HEADS = 4
GROUP = 4
D = 128
ROWS = GROUP * SPAN
LOCAL_SPANS = 128
KEYS = LOCAL_SPANS * SPAN
BLOCK = 1024
CHUNK = 16
FACTOR = math.log2(math.e) / math.sqrt(D)
LOW = -1e30
META = 16
PIECE = 4 * SPAN + META
NT = (((1,), (1,)), ((), ()))
VMEM_SPEC = pl.BlockSpec(memory_space=pltpu.VMEM)
SMEM_SPEC = pl.BlockSpec(memory_space=pltpu.SMEM)
ANY_SPEC = pl.BlockSpec(memory_space=pl.ANY)


def shift(x, axis, by):
    size = 2 if axis == "c" else 4
    return lax.ppermute(x, axis, [(i, (i + by) % size) for i in range(size)])


def prep_kernel(meta_ref, q_ref, k_ref, ks_ref, v_ref, vs_ref, kv_out, q_out):
    rows = k_ref.shape[0]
    row = lax.broadcasted_iota(jnp.int32, (META, 2 * D), 0)
    meta = jnp.zeros((META, 2 * D), F32)
    for r in range(4):
        meta = jnp.where(row == r, meta_ref[r].astype(F32), meta)
    ks, vs = ks_ref[...].astype(F32).T, vs_ref[...].astype(F32).T
    for h in range(HEADS):
        at = slice(h * D, (h + 1) * D)
        kv_out[h, :rows, :D] = (k_ref[:, at].astype(F32) * ks[:, h : h + 1]).astype(BF16)
        kv_out[h, :rows, D:] = (v_ref[:, at].astype(F32) * vs[:, h : h + 1]).astype(BF16)
        kv_out[h, rows:, :] = meta.astype(BF16)
        q_out[h] = q_ref[:, h * GROUP * D : (h + 1) * GROUP * D]


def prep(meta, queries, k, ks, v, vs):
    rows = queries.shape[0]
    return pl.pallas_call(
        prep_kernel,
        out_shape=(
            jax.ShapeDtypeStruct((HEADS, rows + META, 2 * D), BF16),
            jax.ShapeDtypeStruct((HEADS, rows, GROUP * D), BF16),
        ),
        in_specs=[SMEM_SPEC] + [VMEM_SPEC] * 5,
        out_specs=(VMEM_SPEC, VMEM_SPEC),
        name="prep",
    )(meta, queries, k, ks.T, v, vs.T)


def places():
    out = []
    for ab in range(2):
        for dx in range(4):
            for dz in range(4):
                far, near = (dx, dz) if ab == 0 else (dz, dx)
                for y in range(4):
                    row = near * PIECE + y * SPAN
                    if far < 2:
                        out.append((ab * 5 + far, row))
                    elif far == 3:
                        out.append((ab * 5 + 2, row))
                    else:
                        out.append((ab * 5 + 3 + near // 2, row - near // 2 * 2 * PIECE))
    return out


def page_kernel(slot_ref, have_ref, *refs):
    parts, out, sem = refs[:10], refs[10], refs[11]
    for i, (a, row) in enumerate(places()):
        slot = slot_ref[i]

        @pl.when(slot >= 0)
        def _(a=a, row=row, slot=slot):
            pltpu.make_async_copy(parts[a].at[pl.ds(row, SPAN), :], out.at[jnp.maximum(slot, 0)], sem).start()

    for j in range(16):

        @pl.when(have_ref[j] == 0)
        def _(j=j):
            pltpu.make_async_copy(parts[0].at[pl.ds(0, SPAN), :], out.at[j], sem).start()

    pltpu.make_async_copy(out, out, sem).wait()


def pages(slot_of, have, parts):
    return pl.pallas_call(
        page_kernel,
        out_shape=jax.ShapeDtypeStruct((16, SPAN, 2 * D), BF16),
        in_specs=[SMEM_SPEC] * 2 + [ANY_SPEC] * 10,
        out_specs=ANY_SPEC,
        scratch_shapes=[pltpu.SemaphoreType.DMA],
        name="pages",
    )(slot_of, have, *parts)


def attend_kernel(rank_ref, full_ref, qa_ref, qb_ref, *refs):
    parts = refs[:10]
    outs, stats = refs[10:12], refs[12:14]
    (k_s, v_s, q_s, s_a, s_b, p_a, p_b, m_s, al_s, acc, it_q, it_k, sem) = refs[14:]

    for i, (a, row) in enumerate(places()):
        at = pl.ds(pl.multiple_of(rank_ref[i] * SPAN, SPAN), SPAN)
        pltpu.make_async_copy(parts[a].at[pl.ds(row, SPAN), pl.ds(0, D)], k_s.at[at, :], sem.at[0]).start()
        pltpu.make_async_copy(parts[a].at[pl.ds(row, SPAN), pl.ds(D, D)], v_s.at[at, pl.ds(0, D)], sem.at[1]).start()

    v_s[:, D:] = jnp.ones((KEYS, D), BF16)
    for half, q_ref in enumerate((qa_ref, qb_ref)):
        for j in range(8):
            for g in range(GROUP):
                row = (half * 8 + j) * ROWS + g * SPAN
                q_s[row : row + SPAN, :] = q_ref[j * SPAN : (j + 1) * SPAN, g * D : (g + 1) * D]
    q_s[16 * ROWS :, :] = jnp.zeros((ROWS, D), BF16)
    m_s[...] = jnp.full(m_s.shape, LOW, F32)
    acc[...] = jnp.zeros(acc.shape, F32)

    count = jnp.int32(0)
    for j in range(16):
        keys = full_ref[j] * SPAN + (SPAN if j < 8 else 0)
        blocks = (keys + BLOCK - 1) // BLOCK

        def put(b, _, j=j, count=count):
            it_q[count + b] = j
            it_k[count + b] = b
            return 0

        lax.fori_loop(0, blocks, put, 0)
        count = count + blocks
    for extra in range(3):
        it_q[count + extra] = 16
        it_k[count + extra] = 0

    pltpu.make_async_copy(k_s, k_s, sem.at[0]).wait()
    pltpu.make_async_copy(v_s.at[:, pl.ds(0, D)], v_s.at[:, pl.ds(0, D)], sem.at[1]).wait()

    def scores(t, s):
        rows = pl.ds(pl.multiple_of(it_q[t] * ROWS, ROWS), ROWS)
        cols = pl.ds(pl.multiple_of(it_k[t] * BLOCK, BLOCK), BLOCK)
        s[...] = lax.dot_general(q_s[rows, :], k_s[cols, :], NT, preferred_element_type=F32)

    def weigh(t, s, p):
        span = it_q[t]
        first = pl.multiple_of(span * ROWS, ROWS)
        base = full_ref[jnp.minimum(span, 15)] * SPAN - it_k[t] * BLOCK
        own = (span < 8).astype(jnp.int32)
        token = lax.broadcasted_iota(jnp.int32, (CHUNK, D), 0) + 1
        lane = lax.broadcasted_iota(jnp.int32, (CHUNK, D), 1)
        for c in range(ROWS // CHUNK):
            r = slice(c * CHUNK, (c + 1) * CHUNK)
            gap = lane - (base + own * (token + (c * CHUNK) % SPAN))
            tiles = []
            for u in range(BLOCK // D):
                x = s[r, u * D : (u + 1) * D]
                tiles.append(jnp.where(gap < -u * D, x, LOW))
            top = functools.reduce(jnp.maximum, tiles)
            top = jnp.broadcast_to(jnp.max(top, axis=1, keepdims=True), (CHUNK, D)) * FACTOR
            at = pl.ds(first + c * CHUNK, CHUNK)
            old = m_s[at, :]
            new = jnp.maximum(old, top)
            m_s[at, :] = new
            al_s[r, :] = jnp.exp2(old - new)
            for u in range(BLOCK // D):
                p[r, u * D : (u + 1) * D] = jnp.exp2(tiles[u] * FACTOR - new).astype(BF16)

    def gather(t, p):
        rows = pl.ds(pl.multiple_of(it_q[t] * ROWS, ROWS), ROWS)
        cols = pl.ds(pl.multiple_of(it_k[t] * BLOCK, BLOCK), BLOCK)
        o = lax.dot(p[...], v_s[cols, :], preferred_element_type=F32)
        al = al_s[...]
        acc[rows, :] = acc[rows, :] * jnp.concatenate([al, al], axis=1) + o

    scores(0, s_a)

    def body(i, _):
        t = 2 * i
        scores(t + 1, s_b)
        weigh(t, s_a, p_a)
        gather(t, p_a)
        scores(t + 2, s_a)
        weigh(t + 1, s_b, p_b)
        gather(t + 1, p_b)
        return 0

    lax.fori_loop(0, (count + 1) // 2, body, 0)

    lane = lax.broadcasted_iota(jnp.int32, (SPAN, D), 1)
    for half in range(2):
        for j in range(8):
            packed = jnp.zeros((SPAN, D), F32)
            for g in range(GROUP):
                row = (half * 8 + j) * ROWS + g * SPAN
                outs[half][j * SPAN : (j + 1) * SPAN, g * D : (g + 1) * D] = acc[row : row + SPAN, :D]
                packed = jnp.where(lane == g, m_s[row : row + SPAN, :], packed)
                packed = jnp.where(lane == GROUP + g, acc[row : row + SPAN, D:], packed)
            stats[half][j * SPAN : (j + 1) * SPAN, :] = packed


def attend(rank, full, q_own, q_other, parts):
    return pl.pallas_call(
        attend_kernel,
        out_shape=(
            jax.ShapeDtypeStruct((512, 512), F32),
            jax.ShapeDtypeStruct((512, 512), F32),
            jax.ShapeDtypeStruct((512, D), F32),
            jax.ShapeDtypeStruct((512, D), F32),
        ),
        in_specs=[SMEM_SPEC, SMEM_SPEC, VMEM_SPEC, VMEM_SPEC] + [ANY_SPEC] * 10,
        out_specs=(VMEM_SPEC,) * 4,
        scratch_shapes=[
            pltpu.VMEM((KEYS, D), BF16),
            pltpu.VMEM((KEYS, 2 * D), BF16),
            pltpu.VMEM((17 * ROWS, D), BF16),
            pltpu.VMEM((ROWS, BLOCK), F32),
            pltpu.VMEM((ROWS, BLOCK), F32),
            pltpu.VMEM((ROWS, BLOCK), BF16),
            pltpu.VMEM((ROWS, BLOCK), BF16),
            pltpu.VMEM((17 * ROWS, D), F32),
            pltpu.VMEM((ROWS, D), F32),
            pltpu.VMEM((17 * ROWS, 2 * D), F32),
            pltpu.SMEM((16 * (KEYS // BLOCK) + 8,), jnp.int32),
            pltpu.SMEM((16 * (KEYS // BLOCK) + 8,), jnp.int32),
            pltpu.SemaphoreType.DMA((2,)),
        ],
        compiler_params=pltpu.CompilerParams(vmem_limit_bytes=40 * 2**20),
        cost_estimate=pl.CostEstimate(flops=3 * 10**10, bytes_accessed=10**7, transcendentals=0),
        name="attend",
    )(rank, full, q_own, q_other, *parts)


def merge_kernel(oa_ref, sa_ref, ob_ref, sb_ref, out_ref):
    sa, sb = sa_ref[...], sb_ref[...]
    for g in range(GROUP):
        at = slice(g * D, (g + 1) * D)
        ma, mb = sa[:, g : g + 1], sb[:, g : g + 1]
        top = jnp.maximum(ma, mb)
        wa, wb = jnp.exp2(ma - top), jnp.exp2(mb - top)
        total = sa[:, GROUP + g : GROUP + g + 1] * wa + sb[:, GROUP + g : GROUP + g + 1] * wb
        inv = 1.0 / total
        out_ref[:, at] = (oa_ref[:, at] * (wa * inv) + ob_ref[:, at] * (wb * inv)).astype(BF16)


def merge(oa, sa, ob, sb):
    return pl.pallas_call(
        merge_kernel,
        out_shape=jax.ShapeDtypeStruct((512, 512), BF16),
        in_specs=[VMEM_SPEC] * 4,
        out_specs=VMEM_SPEC,
        name="merge",
    )(oa, sa, ob, sb)


def local(queries, k, ks, v, vs, span_pos, page_of_slot):
    kv, q = prep(jnp.concatenate([span_pos, page_of_slot]), queries, k, ks, v, vs)
    kv = lax.all_to_all(kv.reshape(4 * (2 * SPAN + META), 2 * D), "y", 0, 0, tiled=True)
    q = lax.all_to_all(q.reshape(512, GROUP * D), "y", 0, 0, tiled=True)
    q_other = shift(q, "c", 1)

    kv = kv.reshape(4, 2 * SPAN + META, 2 * D)
    note = kv[:, 2 * SPAN : 2 * SPAN + 4].reshape(META, 2 * D)
    note_other = shift(note, "c", 1)
    a, b = (
        jnp.concatenate([kv[:, i * SPAN : (i + 1) * SPAN].reshape(4 * SPAN, 2 * D), note])
        for i in range(2)
    )
    a = jnp.concatenate([a, shift(a, "z", -1), shift(a, "z", 2), shift(a, "z", 1)], axis=0)
    b = jnp.concatenate([b, shift(b, X, -1), shift(b, X, 2), shift(b, X, 1)], axis=0)
    a_next, a_prev = shift(a, X, -1), shift(a, X, 1)
    b_next, b_prev = shift(b, "z", -1), shift(b, "z", 1)
    a_far = shift(a_prev[: 2 * PIECE], X, 1), shift(a_next[2 * PIECE :], X, -1)
    b_far = shift(b_prev[: 2 * PIECE], "z", 1), shift(b_next[2 * PIECE :], "z", -1)
    parts = (a, a_next, a_prev, *a_far, b, b_next, b_prev, *b_far)

    def notes(x):
        return x.reshape(-1, PIECE, 2 * D)[:, 4 * SPAN :, 0]

    every = jnp.concatenate([notes(x) for x in (a, a_next, *a_far, a_prev)], axis=0)
    every = every.astype(jnp.int32).reshape(4, 4, 4, 4)
    own = every[0, 0]
    other = note_other[:, 0].astype(jnp.int32).reshape(4, 4)
    pos = every[..., :2].transpose(3, 0, 1, 2).reshape(LOCAL_SPANS)
    q_pos = jnp.concatenate([own[:, :2].reshape(8), other[:, :2].reshape(8)])
    slot_page = jnp.concatenate([own[:, 2:].reshape(8), other[:, 2:].reshape(8)])
    rank = jnp.sum((pos[None, :] < pos[:, None]).astype(jnp.int32), axis=1)
    full = jnp.sum((pos[None, :] < q_pos[:, None]).astype(jnp.int32), axis=1)
    hit = slot_page[None, :] == pos[:, None]
    slot_of = jnp.sum(jnp.where(hit, jnp.arange(1, 17, dtype=jnp.int32)[None, :], 0), axis=1) - 1
    have = jnp.any(hit, axis=0)

    page = pages(slot_of, have.astype(jnp.int32), parts)
    page_in = shift(page[8:], "c", 1)
    page = jnp.where(have[:8, None, None], page[:8], page_in)
    page = lax.all_to_all(page.reshape(8 * SPAN, 2 * D), "y", 0, 0, tiled=True)
    page = page.reshape(HEADS, 2, SPAN, 2, D).transpose(3, 1, 2, 0, 4).reshape(2, 2, SPAN, HEADS * D)

    o_own, o_other, s_own, s_other = attend(rank, full, q, q_other, parts)
    o_in, s_in = shift(o_other, "c", 1), shift(s_other, "c", 1)
    out = merge(o_own, s_own, o_in, s_in)
    out = lax.all_to_all(out, "y", 0, 1, tiled=True)
    return out, page[0], page[1]


def solution(mesh):
    fine = Mesh(mesh.devices.reshape(2, 4, 2, 4, 2), AXES)
    rows, flat = P(AXES, None), P(AXES)
    return jax.shard_map(
        local,
        mesh=fine,
        in_specs=(rows, rows, rows, rows, rows, flat, flat),
        out_specs=(rows, P(AXES, None, None), P(AXES, None, None)),
        check_vma=False,
    )
```

```python
import functools
import math

import jax
import jax.numpy as jnp
from jax import lax
from jax.experimental import pallas as pl
from jax.experimental.pallas import tpu as pltpu
from jax.sharding import Mesh
from jax.sharding import PartitionSpec as P

AXES = ("xh", "z", "c", "y", "xl")
X = ("xh", "xl")
BF16 = jnp.bfloat16
F32 = jnp.float32
SPAN = 64
HEADS = 4
GROUP = 4
D = 128
ROWS = GROUP * SPAN
BLOCK = 1024
PER = BLOCK // SPAN
PAIR = 2 * ROWS
CHUNK = 16
FACTOR = math.log2(math.e) / math.sqrt(D)
LOW = -1e30
META = 16
PIECE = 4 * SPAN + META
PAGE = GROUP * D + D
PACK = 2 * SPAN + META + 4 * SPAN
RANK, FULL, TURN, SLOT, HAVE = range(5)
NT = (((1,), (1,)), ((), ()))
VMEM_SPEC = pl.BlockSpec(memory_space=pltpu.VMEM)
SMEM_SPEC = pl.BlockSpec(memory_space=pltpu.SMEM)
ANY_SPEC = pl.BlockSpec(memory_space=pl.ANY)


SMALL = pltpu.CompilerParams(vmem_limit_bytes=8 * 2**20)
PARAMS = pltpu.CompilerParams(vmem_limit_bytes=24 * 2**20)


def shift(x, axis, by):
    size = 2 if axis == "c" else 4
    return lax.ppermute(x, axis, [(i, (i + by) % size) for i in range(size)])


def cross(x, axis, by):
    if axis == "z":
        axes, at = ("z", "c"), lambda i, c: 2 * i + c
    else:
        axes, at = ("xh", "c", "xl"), lambda i, c: i // 2 * 4 + c * 2 + i % 2
    pairs = [(at(i, c), at((i + by) % 4, 1 - c)) for i in range(4) for c in range(2)]
    return lax.ppermute(x, axes, pairs)


def prep_kernel(pos_ref, slot_ref, q_ref, k_ref, ks_ref, v_ref, vs_ref, out):
    rows = k_ref.shape[0]
    row = lax.broadcasted_iota(jnp.int32, (META, 2 * D), 0)
    meta = jnp.zeros((META, 2 * D), F32)
    for r in range(2):
        meta = jnp.where(row == r, pos_ref[r].astype(F32), meta)
        meta = jnp.where(row == 2 + r, slot_ref[r].astype(F32), meta)
    ks, vs = ks_ref[...].astype(F32).T, vs_ref[...].astype(F32).T
    for h in range(HEADS):
        at = slice(h * D, (h + 1) * D)
        out[h, :rows, :D] = (k_ref[:, at].astype(F32) * ks[:, h : h + 1]).astype(BF16)
        out[h, :rows, D:] = (v_ref[:, at].astype(F32) * vs[:, h : h + 1]).astype(BF16)
        out[h, rows : rows + META, :] = meta.astype(BF16)
        for i in range(2):
            first = rows + META + i * rows
            at = slice((h * 2 + i) * 2 * D, (h * 2 + i + 1) * 2 * D)
            out[h, first : first + rows, :] = q_ref[:, at]


def prep(pos, slot, queries, k, ks, v, vs):
    return pl.pallas_call(
        prep_kernel,
        out_shape=jax.ShapeDtypeStruct((HEADS, PACK, 2 * D), BF16),
        in_specs=[SMEM_SPEC] * 2 + [VMEM_SPEC] * 5,
        out_specs=VMEM_SPEC,
        name="prep",
    )(pos, slot, queries, k, ks.T, v, vs.T)


def split_kernel(x_ref, a_ref, b_ref, q_ref, note_ref):
    note = jnp.concatenate([x_ref[y, 2 * SPAN : 2 * SPAN + META, :].astype(F32)[:4] for y in range(4)], axis=0)
    note = note.astype(BF16)
    note_ref[...] = note
    for i, ref in enumerate((a_ref, b_ref)):
        for y in range(4):
            ref[y * SPAN : (y + 1) * SPAN, :] = x_ref[y, i * SPAN : (i + 1) * SPAN, :]
        ref[4 * SPAN :, :] = note
    rows = 2 * SPAN
    for y in range(4):
        for i in range(2):
            first = rows + META + i * rows
            q_ref[y * rows : (y + 1) * rows, i * 2 * D : (i + 1) * 2 * D] = x_ref[y, first : first + rows, :]


def split(x):
    return pl.pallas_call(
        split_kernel,
        out_shape=(
            jax.ShapeDtypeStruct((PIECE, 2 * D), BF16),
            jax.ShapeDtypeStruct((PIECE, 2 * D), BF16),
            jax.ShapeDtypeStruct((8 * SPAN, GROUP * D), BF16),
            jax.ShapeDtypeStruct((META, 2 * D), BF16),
        ),
        in_specs=[VMEM_SPEC],
        out_specs=(VMEM_SPEC,) * 4,
        compiler_params=SMALL,
        name="split",
    )(x)


def copy_kernel(moves, inputs, *refs):
    ins, rest = refs[:inputs], refs[inputs:]
    outs, sem = rest[:-1], rest[-1]
    copies = [
        pltpu.make_async_copy(ins[i].at[pl.ds(a, n), :], outs[o].at[pl.ds(b, n), :], sem.at[c])
        for c, (i, a, o, b, n) in enumerate(moves)
    ]
    for copy in copies:
        copy.start()
    for copy in copies:
        copy.wait()


def move(name, moves, rows, *arrays):
    return pl.pallas_call(
        functools.partial(copy_kernel, moves, len(arrays)),
        out_shape=tuple(jax.ShapeDtypeStruct((r, 2 * D), BF16) for r in rows),
        in_specs=[ANY_SPEC] * len(arrays),
        out_specs=(VMEM_SPEC,) * len(rows),
        scratch_shapes=[pltpu.SemaphoreType.DMA((len(moves),))],
        compiler_params=SMALL,
        name=name,
    )(*arrays)


def offsets(pieces):
    return [p * PIECE + y * SPAN for p in range(pieces) for y in range(4)]


def load_parts(parts, kv_s, sem):
    copies, row = [], 0
    for i, part in enumerate(parts):
        copies.append(pltpu.make_async_copy(part, kv_s.at[pl.ds(row, part.shape[0]), :], sem.at[i]))
        row += part.shape[0]
    for copy in copies:
        copy.start()
    return copies


def tables(kinds, kv_s, note_refs, tab_v, tab, sem, have=None):
    count = len(kinds) * 4
    row = lax.broadcasted_iota(jnp.int32, (META, D), 0)
    lane = lax.broadcasted_iota(jnp.int32, (META, D), 1)
    place = jnp.zeros((1, D), F32)
    for p, kind in enumerate(kinds):
        x = kv_s[p * PIECE + 4 * SPAN : (p + 1) * PIECE, :D].astype(F32)
        hit = jnp.logical_and(row == (lane - p * 4) * 4 + kind, jnp.logical_and(lane >= p * 4, lane < p * 4 + 4))
        place = place + jnp.sum(jnp.where(hit, x, 0.0), axis=0, keepdims=True)
    q_place, slot = jnp.zeros((1, D), F32), jnp.zeros((1, D), F32)
    for half, ref in enumerate(note_refs):
        x = ref[:, :D].astype(F32)
        j = lane - half * 8
        hit = jnp.logical_and(jnp.logical_and(j >= 0, j < 8), row == (j // 2) * 4 + j % 2)
        q_place = q_place + jnp.sum(jnp.where(hit, x, 0.0), axis=0, keepdims=True)
        hit = jnp.logical_and(jnp.logical_and(j >= 0, j < 8), row == (j // 2) * 4 + j % 2 + 2)
        slot = slot + jnp.sum(jnp.where(hit, x, 0.0), axis=0, keepdims=True)
    big_row = lax.broadcasted_iota(jnp.int32, (D, D), 0)
    down = jnp.broadcast_to(place, (D, D)).T
    inside = big_row < count

    def below(x, limit, where):
        return jnp.sum(jnp.where(jnp.logical_and(x < limit, where), 1.0, 0.0), axis=0, keepdims=True).astype(jnp.int32)

    tab_v[RANK : RANK + 1, :] = below(down, place, inside)
    tab_v[FULL : FULL + 1, :] = below(down, q_place, inside)
    q_down = jnp.broadcast_to(q_place, (D, D)).T
    big_lane = lax.broadcasted_iota(jnp.int32, (D, D), 1)
    same = jnp.logical_and(big_row // 8 == big_lane // 8, big_row < 8 * len(note_refs))
    tab_v[TURN : TURN + 1, :] = below(q_down, q_place, same) + lane[:1] // 8 * 8
    at = ((big_row // 4) * PIECE + big_row % 4 * SPAN + 1).astype(F32)
    hit = jnp.logical_and(down == slot, inside)
    tab_v[SLOT : SLOT + 1, :] = jnp.sum(jnp.where(hit, at, 0.0), axis=0, keepdims=True).astype(jnp.int32) - 1
    if have is not None:
        tab_v[HAVE : HAVE + 1, :] = have[...]
    copy = pltpu.make_async_copy(tab_v, tab, sem)
    copy.start()
    copy.wait()


def place_queries(q_refs, tab, q_s):
    for half, q_ref in enumerate(q_refs):
        for j in range(8):
            first = tab[TURN, half * 8 + j] * ROWS
            for g in range(GROUP):
                at = pl.ds(pl.multiple_of(first + g * SPAN, SPAN), SPAN)
                q_s[at, :] = q_ref[j * SPAN : (j + 1) * SPAN, g * D : (g + 1) * D]


def flash(spans, count, diagonal, tab, q_s, kv_s, m_s, acc, work):
    s_a, s_b, p_a, p_b, al_a, al_b, order, full_s, own_s, it_q, it_k, it_sub = work
    for i, row in enumerate(offsets(spans // 4)):
        order[tab[RANK, i]] = row
    for j in range(count):
        full_s[tab[TURN, j]] = tab[FULL, j] * SPAN
        own_s[tab[TURN, j]] = 1 if diagonal and j < 8 else 0

    total = jnp.int32(0)
    for pair in range(count // 2):
        keys = jnp.maximum(
            full_s[2 * pair] + own_s[2 * pair] * SPAN,
            full_s[2 * pair + 1] + own_s[2 * pair + 1] * SPAN,
        )
        blocks = (keys + BLOCK - 1) // BLOCK

        def put(b, _, pair=pair, total=total):
            it_q[total + b] = pair
            it_k[total + b] = b * PER
            it_sub[total + b] = b * BLOCK
            return 0

        lax.fori_loop(0, blocks, put, 0)
        total = total + blocks
    for extra in range(3):
        it_q[total + extra] = 0
        it_k[total + extra] = 0
        it_sub[total + extra] = 1 << 20

    def rows_of(t):
        return pl.ds(pl.multiple_of(it_q[t] * PAIR, PAIR), PAIR)

    def keys_of(t, lanes):
        first = it_k[t]
        return jnp.concatenate(
            [kv_s[pl.ds(pl.multiple_of(order[first + i], 16), SPAN), lanes] for i in range(PER)], axis=0
        )

    def scores(t, s):
        s[...] = lax.dot_general(
            q_s[rows_of(t), :], keys_of(t, slice(0, D)), NT, preferred_element_type=F32
        )

    def weigh(t, s, p, al):
        first = pl.multiple_of(it_q[t] * PAIR, PAIR)
        token = lax.broadcasted_iota(jnp.int32, (CHUNK, D), 0) + 1
        lane = lax.broadcasted_iota(jnp.int32, (CHUNK, D), 1)
        for c in range(PAIR // CHUNK):
            r = slice(c * CHUNK, (c + 1) * CHUNK)
            which = it_q[t] * 2 + c * CHUNK // ROWS
            limit = full_s[which] - it_sub[t]
            if diagonal:
                limit = limit + own_s[which] * (token + (c * CHUNK) % SPAN)
            tiles = []
            for u in range(BLOCK // D):
                x = s[r, u * D : (u + 1) * D]
                tiles.append(jnp.where(lane < limit - u * D, x, LOW))
            top = functools.reduce(jnp.maximum, tiles)
            top = jnp.broadcast_to(jnp.max(top, axis=1, keepdims=True), (CHUNK, D)) * FACTOR
            at = pl.ds(first + c * CHUNK, CHUNK)
            old = m_s[at, :]
            new = jnp.maximum(old, top)
            m_s[at, :] = new
            al[r, :] = jnp.exp2(old - new)
            for u in range(BLOCK // D):
                p[r, u * D : (u + 1) * D] = jnp.exp2(tiles[u] * FACTOR - new).astype(BF16)

    def gather(t, p, al_ref):
        v = keys_of(t, slice(D, 2 * D))
        v = jnp.concatenate([v, jnp.ones((BLOCK, D), BF16)], axis=1)
        o = lax.dot(p[...], v, preferred_element_type=F32)
        al = al_ref[...]
        rows = rows_of(t)
        acc[rows, :] = acc[rows, :] * jnp.concatenate([al, al], axis=1) + o

    scores(0, s_a)

    def body(i, _):
        t = 2 * i
        scores(t + 1, s_b)
        weigh(t, s_a, p_a, al_a)
        gather(t, p_a, al_a)
        scores(t + 2, s_a)
        weigh(t + 1, s_b, p_b, al_b)
        gather(t + 1, p_b, al_b)
        return 0

    lax.fori_loop(0, (total + 1) // 2, body, 0)


def work_shapes(spans, count):
    items = count // 2 * (spans // PER + 1) + 8
    return [
        pltpu.VMEM((PAIR, BLOCK), F32),
        pltpu.VMEM((PAIR, BLOCK), F32),
        pltpu.VMEM((PAIR, BLOCK), BF16),
        pltpu.VMEM((PAIR, BLOCK), BF16),
        pltpu.VMEM((PAIR, D), F32),
        pltpu.VMEM((PAIR, D), F32),
        pltpu.SMEM((spans + PER,), jnp.int32),
        pltpu.SMEM((count,), jnp.int32),
        pltpu.SMEM((count,), jnp.int32),
        pltpu.SMEM((items,), jnp.int32),
        pltpu.SMEM((items,), jnp.int32),
        pltpu.SMEM((items,), jnp.int32),
    ]


def scratch(spans, count, parts):
    return [
        pltpu.VMEM((spans // 4 * PIECE, 2 * D), BF16),
        pltpu.VMEM((count * ROWS, D), BF16),
        pltpu.SemaphoreType.DMA((parts,)),
        pltpu.VMEM((8, D), jnp.int32),
        pltpu.SMEM((8, D), jnp.int32),
        pltpu.SemaphoreType.DMA,
    ] + work_shapes(spans, count)


def chunk_row(tab, j):
    return pl.ds(pl.multiple_of(jnp.maximum(tab[SLOT, j], 0), 16), SPAN)


def first_kernel(na_ref, nb_ref, qa_ref, qb_ref, *refs):
    parts, (m_s, acc, page, have), rest = refs[:2], refs[2:6], refs[6:]
    kv_s, q_s, sem, tab_v, tab, tab_sem, *work = rest
    copies = load_parts(parts, kv_s, sem)
    m_s[...] = jnp.full(m_s.shape, LOW, F32)
    acc[...] = jnp.zeros(acc.shape, F32)
    for copy in copies:
        copy.wait()
    tables((0,) * 4 + (1,) * 4, kv_s, (na_ref, nb_ref), tab_v, tab, tab_sem)
    have[...] = tab_v[SLOT : SLOT + 1, :]
    for j in range(16):
        page[j] = kv_s[chunk_row(tab, j), :]
    place_queries((qa_ref, qb_ref), tab, q_s)
    flash(32, 16, True, tab, q_s, kv_s, m_s, acc, work)


def give_kernel(note_ref, q_ref, m_in, acc_in, page_in, *refs):
    parts, give, rest = refs[:4], refs[4], refs[5:]
    m_s, acc, kv_s, q_s, sem, tab_v, tab, tab_sem, *work = rest
    copies = load_parts(parts, kv_s, sem)
    m_s[...] = m_in[8 * ROWS :, :]
    acc[...] = acc_in[8 * ROWS :, :]
    for copy in copies:
        copy.wait()
    tables((0,) * 8 + (1,) * 8, kv_s, (note_ref,), tab_v, tab, tab_sem)
    place_queries((q_ref,), tab, q_s)
    flash(64, 8, False, tab, q_s, kv_s, m_s, acc, work)
    lane = lax.broadcasted_iota(jnp.int32, (SPAN, D), 1)
    for j in range(8):
        at = slice(j * SPAN, (j + 1) * SPAN)
        packed = jnp.zeros((SPAN, D), F32)
        for g in range(GROUP):
            rows = pl.ds(pl.multiple_of(tab[TURN, j] * ROWS + g * SPAN, SPAN), SPAN)
            give[at, g * D : (g + 1) * D] = acc[rows, :D]
            packed = jnp.where(lane == g, m_s[rows, :], packed)
            packed = jnp.where(lane == GROUP + g, acc[rows, D:], packed)
        give[at, GROUP * D : PAGE] = packed
        found = tab[SLOT, j] >= 0
        give[at, PAGE:] = jnp.where(found, kv_s[chunk_row(tab, j), :].astype(F32), page_in[8 + j].astype(F32))


def second_kernel(note_ref, q_ref, m_in, acc_in, page_in, have_in, *refs):
    parts, (m_s, acc, page, have), rest = refs[:4], refs[4:8], refs[8:]
    kv_s, q_s, sem, tab_v, tab, tab_sem, *work = rest
    copies = load_parts(parts, kv_s, sem)
    m_s[...] = m_in[: 8 * ROWS, :]
    acc[...] = acc_in[: 8 * ROWS, :]
    for copy in copies:
        copy.wait()
    tables((0,) * 8 + (1,) * 8, kv_s, (note_ref,), tab_v, tab, tab_sem)
    have[...] = jnp.maximum(have_in[...], tab_v[SLOT : SLOT + 1, :])
    for j in range(8):
        page[j] = jnp.where(tab[SLOT, j] >= 0, kv_s[chunk_row(tab, j), :].astype(F32), page_in[j].astype(F32)).astype(BF16)
    place_queries((q_ref,), tab, q_s)
    flash(64, 8, False, tab, q_s, kv_s, m_s, acc, work)


def third_kernel(note_ref, have, q_ref, m_in, acc_in, take, page, *refs):
    parts, out, rest = refs[:4], refs[4], refs[5:]
    m_s, acc, kv_s, q_s, sem, tab_v, tab, tab_sem, *work = rest
    copies = load_parts(parts, kv_s, sem)
    for copy in copies:
        copy.wait()
    tables(((0,) * 4 + (1,) * 4) * 2, kv_s, (note_ref,), tab_v, tab, tab_sem, have)
    place_queries((q_ref,), tab, q_s)
    for j in range(8):
        at = slice(j * SPAN, (j + 1) * SPAN)
        for g in range(GROUP):
            rows = pl.ds(pl.multiple_of(tab[TURN, j] * ROWS + g * SPAN, SPAN), SPAN)
            stat = GROUP * D + g
            m_b = jnp.broadcast_to(take[at, stat : stat + 1], (SPAN, D))
            l_b = jnp.broadcast_to(take[at, stat + GROUP : stat + GROUP + 1], (SPAN, D))
            m_a = m_in[rows, :]
            top = jnp.maximum(m_a, m_b)
            w_a, w_b = jnp.exp2(m_a - top), jnp.exp2(m_b - top)
            m_s[rows, :] = top
            acc[rows, :D] = acc_in[rows, :D] * w_a + take[at, g * D : (g + 1) * D] * w_b
            acc[rows, D:] = acc_in[rows, D:] * w_a + l_b * w_b

    for j in range(8):
        y, s = divmod(j, 2)
        far = jnp.where(tab[HAVE, j] >= 0, page[j].astype(F32), take[j * SPAN : (j + 1) * SPAN, PAGE:])
        near = kv_s[chunk_row(tab, j), :].astype(F32)
        out[y, 2 * SPAN :, s * 2 * D : (s + 1) * 2 * D] = jnp.where(tab[SLOT, j] >= 0, near, far).astype(BF16)

    flash(64, 8, False, tab, q_s, kv_s, m_s, acc, work)
    for j in range(8):
        y, ab = divmod(j, 2)
        for g in range(GROUP):
            rows = pl.ds(pl.multiple_of(tab[TURN, j] * ROWS + g * SPAN, SPAN), SPAN)
            out[y, ab * SPAN : (ab + 1) * SPAN, g * D : (g + 1) * D] = (
                acc[rows, :D] * (1.0 / acc[rows, D:])
            ).astype(BF16)


def finish_kernel(x_ref, o_ref, k_ref, v_ref):
    for h in range(HEADS):
        o_ref[:, h * GROUP * D : (h + 1) * GROUP * D] = x_ref[h, : 2 * SPAN, :]
        for s in range(2):
            at = 2 * s * D
            k_ref[s, :, h * D : (h + 1) * D] = x_ref[h, 2 * SPAN :, at : at + D]
            v_ref[s, :, h * D : (h + 1) * D] = x_ref[h, 2 * SPAN :, at + D : at + 2 * D]


def cost(scores):
    return pl.CostEstimate(flops=scores * 2048, bytes_accessed=2**20, transcendentals=0)


HAVE_SHAPE = jax.ShapeDtypeStruct((1, D), jnp.int32)


def state_shape(count):
    return [jax.ShapeDtypeStruct((count * ROWS, D), F32), jax.ShapeDtypeStruct((count * ROWS, 2 * D), F32)]


STATE = [pltpu.VMEM((8 * ROWS, D), F32), pltpu.VMEM((8 * ROWS, 2 * D), F32)]


def first(notes, q, q_other, parts):
    return pl.pallas_call(
        first_kernel,
        out_shape=(*state_shape(16), jax.ShapeDtypeStruct((16, SPAN, 2 * D), BF16), HAVE_SHAPE),
        in_specs=[VMEM_SPEC] * 4 + [ANY_SPEC] * 2,
        out_specs=(VMEM_SPEC,) * 4,
        scratch_shapes=scratch(32, 16, 2),
        compiler_params=PARAMS,
        cost_estimate=cost(16 * ROWS * 1024),
        name="first",
    )(*notes, q, q_other, *parts)


def give(note, q, m, acc, page, parts):
    return pl.pallas_call(
        give_kernel,
        out_shape=jax.ShapeDtypeStruct((8 * SPAN, PAGE + 2 * D), F32),
        in_specs=[VMEM_SPEC] * 5 + [ANY_SPEC] * 4,
        out_specs=VMEM_SPEC,
        scratch_shapes=STATE + scratch(64, 8, 4),
        compiler_params=PARAMS,
        cost_estimate=cost(8 * ROWS * 2048),
        name="give",
    )(note, q, m, acc, page, *parts)


def second(note, q, m, acc, page, have, parts):
    return pl.pallas_call(
        second_kernel,
        out_shape=(*state_shape(8), jax.ShapeDtypeStruct((8, SPAN, 2 * D), BF16), HAVE_SHAPE),
        in_specs=[VMEM_SPEC] * 6 + [ANY_SPEC] * 4,
        out_specs=(VMEM_SPEC,) * 4,
        scratch_shapes=scratch(64, 8, 4),
        compiler_params=PARAMS,
        cost_estimate=cost(8 * ROWS * 2048),
        name="second",
    )(note, q, m, acc, page, have, *parts)


def third(note, have, q, m, acc, take, page, parts):
    return pl.pallas_call(
        third_kernel,
        out_shape=jax.ShapeDtypeStruct((4, 3 * SPAN, GROUP * D), BF16),
        in_specs=[VMEM_SPEC] * 7 + [ANY_SPEC] * 4,
        out_specs=VMEM_SPEC,
        scratch_shapes=STATE + scratch(64, 8, 4),
        compiler_params=PARAMS,
        cost_estimate=cost(8 * ROWS * 2048),
        name="third",
    )(note, have, q, m, acc, take, page, *parts)


def finish(x):
    return pl.pallas_call(
        finish_kernel,
        out_shape=(
            jax.ShapeDtypeStruct((2 * SPAN, HEADS * GROUP * D), BF16),
            jax.ShapeDtypeStruct((2, SPAN, HEADS * D), BF16),
            jax.ShapeDtypeStruct((2, SPAN, HEADS * D), BF16),
        ),
        in_specs=[VMEM_SPEC],
        out_specs=(VMEM_SPEC,) * 3,
        compiler_params=SMALL,
        name="finish",
    )(x)


def local(queries, k, ks, v, vs, span_pos, page_of_slot):
    pack = prep(span_pos, page_of_slot, queries, k, ks, v, vs)
    pack = lax.all_to_all(pack.reshape(HEADS * PACK, 2 * D), "y", 0, 0, tiled=True)
    a, b, q, note = split(pack.reshape(4, PACK, 2 * D))
    q_other, note_other = shift(q, "c", 1), shift(note, "c", 1)
    notes = (note, note_other)

    a1, a2, a3 = shift(a, "z", -1), shift(a, "z", 2), shift(a, "z", 1)
    b1, b2, b3 = shift(b, X, -1), shift(b, X, 2), shift(b, X, 1)
    b3, q_other = lax.optimization_barrier((b3, q_other))
    moves = [(i, 0, i // 4, i % 4 * PIECE, PIECE) for i in range(8)]
    a, b = move("join", moves, (4 * PIECE, 4 * PIECE), a, a1, a2, a3, b, b1, b2, b3)
    a_next, a_prev = shift(a, X, -1), shift(a, X, 1)
    b_next, b_prev = shift(b, "z", -1), shift(b, "z", 1)

    m, acc, page, have = first(notes, q, q_other, (a, b))

    near = (a_next, a_prev, b_next, b_prev)
    near, m, acc, page, have = lax.optimization_barrier((near, m, acc, page, have))
    a_next, a_prev, b_next, b_prev = near
    far = (shift(a_prev, X, 1), shift(b_prev, "z", 1), cross(a_next, X, -1), cross(b_next, "z", -1))

    take = shift(give(note_other, q_other, m, acc, page, near), "c", 1)
    m, acc, page, have = second(note, q, m, acc, page, have, near)
    out = third(note, have, q, m, acc, take, page, far)
    out = lax.all_to_all(out.reshape(4 * 3 * SPAN, GROUP * D), "y", 0, 0, tiled=True)
    return finish(out.reshape(4, 3 * SPAN, GROUP * D))


def solution(mesh):
    fine = Mesh(mesh.devices.reshape(2, 4, 2, 4, 2), AXES)
    rows, flat = P(AXES, None), P(AXES)
    return jax.shard_map(
        local,
        mesh=fine,
        in_specs=(rows, rows, rows, rows, rows, flat, flat),
        out_specs=(rows, P(AXES, None, None), P(AXES, None, None)),
        check_vma=False,
    )
```

```python
import functools
import math

import jax
import jax.numpy as jnp
from jax import lax
from jax.experimental import pallas as pl
from jax.experimental.pallas import tpu as pltpu
from jax.sharding import Mesh
from jax.sharding import PartitionSpec as P

AXES = ("xh", "z", "c", "y", "xl")
X = ("xh", "xl")
BF16 = jnp.bfloat16
F32 = jnp.float32
SPAN = 64
HEADS = 4
GROUP = 4
D = 128
ROWS = GROUP * SPAN
BLOCK = 1024
PER = BLOCK // SPAN
PAIR = 2 * ROWS
CHUNK = 16
FACTOR = math.log2(math.e) / math.sqrt(D)
LOW = -1e30
META = 16
PIECE = 4 * SPAN + META
PACK = 2 * SPAN + META + 4 * SPAN
RANK, FULL, TURN, SLOT = range(4)
NT = (((1,), (1,)), ((), ()))
VMEM_SPEC = pl.BlockSpec(memory_space=pltpu.VMEM)
SMEM_SPEC = pl.BlockSpec(memory_space=pltpu.SMEM)
ANY_SPEC = pl.BlockSpec(memory_space=pl.ANY)


SMALL = pltpu.CompilerParams(vmem_limit_bytes=8 * 2**20)
PARAMS = pltpu.CompilerParams(vmem_limit_bytes=24 * 2**20)


def shift(x, axis, by):
    size = 2 if axis == "c" else 4
    return lax.ppermute(x, axis, [(i, (i + by) % size) for i in range(size)])


def cross(x, axis, by):
    if axis == "z":
        axes, at = ("z", "c"), lambda i, c: 2 * i + c
    else:
        axes, at = ("xh", "c", "xl"), lambda i, c: i // 2 * 4 + c * 2 + i % 2
    pairs = [(at(i, c), at((i + by) % 4, 1 - c)) for i in range(4) for c in range(2)]
    return lax.ppermute(x, axes, pairs)


def prep_kernel(pos_ref, slot_ref, q_ref, k_ref, ks_ref, v_ref, vs_ref, out):
    rows = k_ref.shape[0]
    row = lax.broadcasted_iota(jnp.int32, (META, 2 * D), 0)
    meta = jnp.zeros((META, 2 * D), F32)
    for r in range(2):
        meta = jnp.where(row == r, pos_ref[r].astype(F32), meta)
        meta = jnp.where(row == 2 + r, slot_ref[r].astype(F32), meta)
    ks, vs = ks_ref[...].astype(F32).T, vs_ref[...].astype(F32).T
    for h in range(HEADS):
        at = slice(h * D, (h + 1) * D)
        out[h, :rows, :D] = (k_ref[:, at].astype(F32) * ks[:, h : h + 1]).astype(BF16)
        out[h, :rows, D:] = (v_ref[:, at].astype(F32) * vs[:, h : h + 1]).astype(BF16)
        out[h, rows : rows + META, :] = meta.astype(BF16)
        for i in range(2):
            first = rows + META + i * rows
            at = slice((h * 2 + i) * 2 * D, (h * 2 + i + 1) * 2 * D)
            out[h, first : first + rows, :] = q_ref[:, at]


def prep(pos, slot, queries, k, ks, v, vs):
    return pl.pallas_call(
        prep_kernel,
        out_shape=jax.ShapeDtypeStruct((HEADS, PACK, 2 * D), BF16),
        in_specs=[SMEM_SPEC] * 2 + [VMEM_SPEC] * 5,
        out_specs=VMEM_SPEC,
        name="prep",
    )(pos, slot, queries, k, ks.T, v, vs.T)


def split_kernel(x_ref, a_ref, b_ref, q_ref, note_ref):
    note = jnp.concatenate([x_ref[y, 2 * SPAN : 2 * SPAN + META, :].astype(F32)[:4] for y in range(4)], axis=0)
    note = note.astype(BF16)
    note_ref[...] = note
    for i, ref in enumerate((a_ref, b_ref)):
        for y in range(4):
            ref[y * SPAN : (y + 1) * SPAN, :] = x_ref[y, i * SPAN : (i + 1) * SPAN, :]
        ref[4 * SPAN :, :] = note
    rows = 2 * SPAN
    for y in range(4):
        for i in range(2):
            first = rows + META + i * rows
            q_ref[y * rows : (y + 1) * rows, i * 2 * D : (i + 1) * 2 * D] = x_ref[y, first : first + rows, :]


def split(x):
    return pl.pallas_call(
        split_kernel,
        out_shape=(
            jax.ShapeDtypeStruct((PIECE, 2 * D), BF16),
            jax.ShapeDtypeStruct((PIECE, 2 * D), BF16),
            jax.ShapeDtypeStruct((8 * SPAN, GROUP * D), BF16),
            jax.ShapeDtypeStruct((META, 2 * D), BF16),
        ),
        in_specs=[VMEM_SPEC],
        out_specs=(VMEM_SPEC,) * 4,
        compiler_params=SMALL,
        name="split",
    )(x)


def copy_kernel(moves, inputs, *refs):
    ins, rest = refs[:inputs], refs[inputs:]
    outs, sem = rest[:-1], rest[-1]
    copies = [
        pltpu.make_async_copy(ins[i].at[pl.ds(a, n), :], outs[o].at[pl.ds(b, n), :], sem.at[c])
        for c, (i, a, o, b, n) in enumerate(moves)
    ]
    for copy in copies:
        copy.start()
    for copy in copies:
        copy.wait()


def move(name, moves, rows, *arrays):
    return pl.pallas_call(
        functools.partial(copy_kernel, moves, len(arrays)),
        out_shape=tuple(jax.ShapeDtypeStruct((r, 2 * D), BF16) for r in rows),
        in_specs=[ANY_SPEC] * len(arrays),
        out_specs=(VMEM_SPEC,) * len(rows),
        scratch_shapes=[pltpu.SemaphoreType.DMA((len(moves),))],
        compiler_params=SMALL,
        name=name,
    )(*arrays)


def offsets(pieces):
    return [p * PIECE + y * SPAN for p in range(pieces) for y in range(4)]


def load_parts(parts, kv_s, sem):
    copies, row = [], 0
    for i, part in enumerate(parts):
        copies.append(pltpu.make_async_copy(part, kv_s.at[pl.ds(row, part.shape[0]), :], sem.at[i]))
        row += part.shape[0]
    for copy in copies:
        copy.start()
    return copies


def tables(kinds, kv_s, note_refs, tab_v, tab, sem):
    count = len(kinds) * 4
    row = lax.broadcasted_iota(jnp.int32, (META, D), 0)
    lane = lax.broadcasted_iota(jnp.int32, (META, D), 1)
    place = jnp.zeros((1, D), F32)
    for p, kind in enumerate(kinds):
        x = kv_s[p * PIECE + 4 * SPAN : (p + 1) * PIECE, :D].astype(F32)
        hit = jnp.logical_and(row == (lane - p * 4) * 4 + kind, jnp.logical_and(lane >= p * 4, lane < p * 4 + 4))
        place = place + jnp.sum(jnp.where(hit, x, 0.0), axis=0, keepdims=True)
    q_place, slot = jnp.zeros((1, D), F32), jnp.zeros((1, D), F32)
    for half, ref in enumerate(note_refs):
        x = ref[:, :D].astype(F32)
        j = lane - half * 8
        hit = jnp.logical_and(jnp.logical_and(j >= 0, j < 8), row == (j // 2) * 4 + j % 2)
        q_place = q_place + jnp.sum(jnp.where(hit, x, 0.0), axis=0, keepdims=True)
        hit = jnp.logical_and(jnp.logical_and(j >= 0, j < 8), row == (j // 2) * 4 + j % 2 + 2)
        slot = slot + jnp.sum(jnp.where(hit, x, 0.0), axis=0, keepdims=True)
    big_row = lax.broadcasted_iota(jnp.int32, (D, D), 0)
    down = jnp.broadcast_to(place, (D, D)).T
    inside = big_row < count

    def below(x, limit, where):
        return jnp.sum(jnp.where(jnp.logical_and(x < limit, where), 1.0, 0.0), axis=0, keepdims=True).astype(jnp.int32)

    tab_v[RANK : RANK + 1, :] = below(down, place, inside)
    tab_v[FULL : FULL + 1, :] = below(down, q_place, inside)
    q_down = jnp.broadcast_to(q_place, (D, D)).T
    big_lane = lax.broadcasted_iota(jnp.int32, (D, D), 1)
    same = jnp.logical_and(big_row // 8 == big_lane // 8, big_row < 8 * len(note_refs))
    tab_v[TURN : TURN + 1, :] = below(q_down, q_place, same) + lane[:1] // 8 * 8
    at = ((big_row // 4) * PIECE + big_row % 4 * SPAN + 1).astype(F32)
    hit = jnp.logical_and(down == slot, inside)
    tab_v[SLOT : SLOT + 1, :] = jnp.sum(jnp.where(hit, at, 0.0), axis=0, keepdims=True).astype(jnp.int32) - 1
    copy = pltpu.make_async_copy(tab_v, tab, sem)
    copy.start()
    copy.wait()


def place_queries(q_refs, tab, q_s):
    for half, q_ref in enumerate(q_refs):
        for j in range(8):
            first = tab[TURN, half * 8 + j] * ROWS
            for g in range(GROUP):
                at = pl.ds(pl.multiple_of(first + g * SPAN, SPAN), SPAN)
                q_s[at, :] = q_ref[j * SPAN : (j + 1) * SPAN, g * D : (g + 1) * D]


def flash(spans, count, diagonal, tab, q_s, kv_s, m_s, acc, work):
    s_a, s_b, p_a, p_b, al_a, al_b, hot, order, full_s, own_s, wide, tail = work
    for i, row in enumerate(offsets(spans // 4)):
        order[tab[RANK, i]] = row
    for j in range(count):
        full_s[tab[TURN, j]] = tab[FULL, j]
        own_s[tab[TURN, j]] = 1 if diagonal and j < 8 else 0
    if not diagonal:
        key = lax.broadcasted_iota(jnp.int32, (BLOCK, D), 0)
        hot[...] = jnp.where(lax.broadcasted_iota(jnp.int32, (BLOCK, D), 1) == key // SPAN, 1.0, 0.0).astype(BF16)

    n_wide, n_tail = jnp.int32(0), jnp.int32(0)
    for pair in range(count // 2):
        seen = jnp.maximum(full_s[2 * pair] + own_s[2 * pair], full_s[2 * pair + 1] + own_s[2 * pair + 1])
        rest = lax.rem(seen, PER)
        blocks = lax.div(seen, PER) + (rest > PER // 2).astype(jnp.int32)

        def put(b, _, pair=pair, n_wide=n_wide):
            wide[0, n_wide + b] = pair
            wide[1, n_wide + b] = b * PER
            wide[2, n_wide + b] = b * PER
            return 0

        lax.fori_loop(0, blocks, put, 0)
        n_wide = n_wide + blocks
        tail[0, n_tail] = pair
        tail[1, n_tail] = jnp.minimum(blocks * PER, spans - PER // 2)
        tail[2, n_tail] = blocks * PER
        n_tail = n_tail + jnp.logical_and(rest > 0, rest <= PER // 2).astype(jnp.int32)
    for items, n in ((wide, n_wide), (tail, n_tail)):
        for extra in range(3):
            items[0, n + extra] = 0
            items[1, n + extra] = 0
            items[2, n + extra] = 1 << 20

    def sweep(size, items, total):
        per, cols = size // SPAN, slice(0, size)

        def rows_of(t):
            return pl.ds(pl.multiple_of(items[0, t] * PAIR, PAIR), PAIR)

        def keys_of(t, lanes):
            first = items[1, t]
            return jnp.concatenate(
                [kv_s[pl.ds(pl.multiple_of(order[first + i], 16), SPAN), lanes] for i in range(per)], axis=0
            )

        def scores(t, s):
            q, k = q_s[rows_of(t), :], keys_of(t, slice(0, D))
            if not diagonal:
                lane = lax.broadcasted_iota(jnp.int32, (ROWS, D), 1)
                shut = [
                    jnp.where(lane < full_s[items[0, t] * 2 + i] - items[2, t], 0.0, LOW).astype(BF16)
                    for i in range(2)
                ]
                q = jnp.concatenate([q, jnp.concatenate(shut, axis=0)], axis=1)
                k = jnp.concatenate([k, hot[cols, :]], axis=1)
            s[:, cols] = lax.dot_general(q, k, NT, preferred_element_type=F32)

        def weigh(t, s, p, al):
            first = pl.multiple_of(items[0, t] * PAIR, PAIR)
            token = lax.broadcasted_iota(jnp.int32, (CHUNK, D), 0) + 1
            lane = lax.broadcasted_iota(jnp.int32, (CHUNK, D), 1)
            for c in range(PAIR // CHUNK):
                r = slice(c * CHUNK, (c + 1) * CHUNK)
                tiles = [s[r, u * D : (u + 1) * D] for u in range(size // D)]
                if diagonal:
                    which = items[0, t] * 2 + c * CHUNK // ROWS
                    limit = (full_s[which] - items[2, t]) * SPAN + own_s[which] * (token + (c * CHUNK) % SPAN)
                    gap = lane - limit
                    tiles = [jnp.where(gap < -u * D, x, LOW) for u, x in enumerate(tiles)]
                top = functools.reduce(jnp.maximum, tiles)
                top = jnp.broadcast_to(jnp.max(top, axis=1, keepdims=True), (CHUNK, D)) * FACTOR
                at = pl.ds(first + c * CHUNK, CHUNK)
                old = m_s[at, :]
                new = jnp.maximum(old, top)
                m_s[at, :] = new
                al[r, :] = jnp.exp2(old - new)
                for u, x in enumerate(tiles):
                    p[r, u * D : (u + 1) * D] = jnp.exp2(x * FACTOR - new).astype(BF16)

        def gather(t, p, al_ref):
            v = keys_of(t, slice(D, 2 * D))
            v = jnp.concatenate([v, jnp.ones((size, D), BF16)], axis=1)
            o = lax.dot(p[:, cols], v, preferred_element_type=F32)
            al = al_ref[...]
            rows = rows_of(t)
            acc[rows, :] = acc[rows, :] * jnp.concatenate([al, al], axis=1) + o

        scores(0, s_a)

        def body(i, _):
            t = 2 * i
            scores(t + 1, s_b)
            weigh(t, s_a, p_a, al_a)
            gather(t, p_a, al_a)
            scores(t + 2, s_a)
            weigh(t + 1, s_b, p_b, al_b)
            gather(t + 1, p_b, al_b)
            return 0

        lax.fori_loop(0, (total + 1) // 2, body, 0)

    sweep(BLOCK, wide, n_wide)
    sweep(BLOCK // 2, tail, n_tail)


def work_shapes(spans, count):
    items = count // 2 * (spans // PER + 1) + 8
    return [
        pltpu.VMEM((PAIR, BLOCK), F32),
        pltpu.VMEM((PAIR, BLOCK), F32),
        pltpu.VMEM((PAIR, BLOCK), BF16),
        pltpu.VMEM((PAIR, BLOCK), BF16),
        pltpu.VMEM((PAIR, D), F32),
        pltpu.VMEM((PAIR, D), F32),
        pltpu.VMEM((BLOCK, D), BF16),
        pltpu.SMEM((spans + PER,), jnp.int32),
        pltpu.SMEM((count,), jnp.int32),
        pltpu.SMEM((count,), jnp.int32),
        pltpu.SMEM((3, items), jnp.int32),
        pltpu.SMEM((3, count // 2 + 8), jnp.int32),
    ]


def scratch(spans, count, parts):
    return [
        pltpu.VMEM((spans // 4 * PIECE, 2 * D), BF16),
        pltpu.VMEM((count * ROWS, D), BF16),
        pltpu.SemaphoreType.DMA((parts,)),
        pltpu.VMEM((8, D), jnp.int32),
        pltpu.SMEM((8, D), jnp.int32),
        pltpu.SemaphoreType.DMA,
    ] + work_shapes(spans, count)


def chunk_row(tab, j):
    return pl.ds(pl.multiple_of(jnp.maximum(tab[SLOT, j], 0), 16), SPAN)


def first_kernel(na_ref, nb_ref, qa_ref, qb_ref, *refs):
    parts, (m_s, acc, page, have), rest = refs[:2], refs[2:6], refs[6:]
    kv_s, q_s, sem, tab_v, tab, tab_sem, *work = rest
    copies = load_parts(parts, kv_s, sem)
    m_s[...] = jnp.full(m_s.shape, LOW, F32)
    acc[...] = jnp.zeros(acc.shape, F32)
    for copy in copies:
        copy.wait()
    tables((0,) * 4 + (1,) * 4, kv_s, (na_ref, nb_ref), tab_v, tab, tab_sem)
    have[...] = tab_v[SLOT : SLOT + 1, :]
    for j in range(16):
        page[j] = kv_s[chunk_row(tab, j), :]
    place_queries((qa_ref, qb_ref), tab, q_s)
    flash(32, 16, True, tab, q_s, kv_s, m_s, acc, work)


def give_kernel(note_ref, q_ref, m_in, acc_in, page_in, *refs):
    parts, (give_o, give_p), rest = refs[:4], refs[4:6], refs[6:]
    m_s, acc, levels_s, kv_s, q_s, sem, tab_v, tab, tab_sem, *work = rest
    copies = load_parts(parts, kv_s, sem)
    levels_s[...] = jnp.zeros(levels_s.shape, F32)
    m_s[...] = m_in[8 * ROWS :, :]
    acc[...] = acc_in[8 * ROWS :, :]
    for copy in copies:
        copy.wait()
    tables((0,) * 8 + (1,) * 8, kv_s, (note_ref,), tab_v, tab, tab_sem)
    for j in range(8):
        near = kv_s[chunk_row(tab, j), :].astype(F32)
        give_p[j] = jnp.where(tab[SLOT, j] >= 0, near, page_in[8 + j].astype(F32)).astype(BF16)
    place_queries((q_ref,), tab, q_s)
    flash(64, 8, False, tab, q_s, kv_s, m_s, acc, work)
    for g in range(GROUP):
        for block in range(4):
            logs = []
            for j in (2 * block, 2 * block + 1):
                rows = pl.ds(pl.multiple_of(tab[TURN, j] * ROWS + g * SPAN, SPAN), SPAN)
                sums = jnp.maximum(acc[rows, D:], 1e-30)
                give_o[j * SPAN : (j + 1) * SPAN, g * D : (g + 1) * D] = (acc[rows, :D] * (1.0 / sums)).astype(BF16)
                logs.append(m_s[rows, :] + jnp.log(sums) * math.log2(math.e))
            level = jnp.concatenate(logs, axis=0).T[:1, :]
            for part in range(3):
                piece = level.astype(BF16).astype(F32)
                level = level - piece
                levels_s[part * 4 + g : part * 4 + g + 1, block * D : (block + 1) * D] = piece
    give_o[8 * SPAN :, :] = levels_s[...].astype(BF16)


def own_kernel(note_ref, q_ref, m_in, acc_in, page_in, have, *refs):
    parts, (m_out, acc_out, page, found), rest = refs[:8], refs[8:12], refs[12:]
    m_s, acc, kv_s, q_s, sem, tab_v, tab, tab_sem, *work = rest
    copies = load_parts(parts, kv_s, sem)
    m_s[...] = m_in[: 8 * ROWS, :]
    acc[...] = acc_in[: 8 * ROWS, :]
    for copy in copies:
        copy.wait()
    tables((0,) * 8 + (1,) * 8 + ((0,) * 4 + (1,) * 4) * 2, kv_s, (note_ref,), tab_v, tab, tab_sem)
    found[...] = jnp.maximum(have[...], tab_v[SLOT : SLOT + 1, :])
    for j in range(8):
        near = kv_s[chunk_row(tab, j), :].astype(F32)
        page[j] = jnp.where(tab[SLOT, j] >= 0, near, page_in[j].astype(F32)).astype(BF16)
    place_queries((q_ref,), tab, q_s)
    flash(128, 8, False, tab, q_s, kv_s, m_s, acc, work)
    for j in range(8):
        rows = pl.ds(pl.multiple_of(tab[TURN, j] * ROWS, ROWS), ROWS)
        m_out[j * ROWS : (j + 1) * ROWS, :] = m_s[rows, :]
        acc_out[j * ROWS : (j + 1) * ROWS, :] = acc[rows, :]


def merge_kernel(m_in, acc_in, take, page, found, take_p, out):
    levels = take[8 * SPAN :, :].astype(F32)
    for g in range(GROUP):
        level = levels[g : g + 1] + levels[4 + g : 5 + g] + levels[8 + g : 9 + g]
        for block in range(4):
            both = jnp.broadcast_to(level[:, block * D : (block + 1) * D], (D, D)).T
            for j in (2 * block, 2 * block + 1):
                y, ab = divmod(j, 2)
                rows = slice(j * ROWS + g * SPAN, j * ROWS + (g + 1) * SPAN)
                m_a, m_b = m_in[rows, :], both[j % 2 * SPAN : (j % 2 + 1) * SPAN]
                top = jnp.maximum(m_a, m_b)
                w_a, w_b = jnp.exp2(m_a - top), jnp.exp2(m_b - top)
                o_b = take[j * SPAN : (j + 1) * SPAN, g * D : (g + 1) * D].astype(F32)
                total = acc_in[rows, D:] * w_a + w_b
                o = (acc_in[rows, :D] * w_a + o_b * w_b) * (1.0 / total)
                out[y, ab * SPAN : (ab + 1) * SPAN, g * D : (g + 1) * D] = o.astype(BF16)
    lane = lax.broadcasted_iota(jnp.int32, (1, D), 1)
    for j in range(8):
        y, s = divmod(j, 2)
        here = jnp.max(jnp.where(lane == j, found[...], -1), axis=1, keepdims=True) >= 0
        x = jnp.where(here, page[j].astype(F32), take_p[j].astype(F32))
        out[y, 2 * SPAN :, s * 2 * D : (s + 1) * 2 * D] = x.astype(BF16)


def finish_kernel(x_ref, o_ref, k_ref, v_ref):
    for h in range(HEADS):
        o_ref[:, h * GROUP * D : (h + 1) * GROUP * D] = x_ref[h, : 2 * SPAN, :]
        for s in range(2):
            at = 2 * s * D
            k_ref[s, :, h * D : (h + 1) * D] = x_ref[h, 2 * SPAN :, at : at + D]
            v_ref[s, :, h * D : (h + 1) * D] = x_ref[h, 2 * SPAN :, at + D : at + 2 * D]


def cost(scores):
    return pl.CostEstimate(flops=scores * 2048, bytes_accessed=2**20, transcendentals=0)


HAVE_SHAPE = jax.ShapeDtypeStruct((1, D), jnp.int32)


def state_shape(count):
    return [jax.ShapeDtypeStruct((count * ROWS, D), F32), jax.ShapeDtypeStruct((count * ROWS, 2 * D), F32)]


STATE = [pltpu.VMEM((8 * ROWS, D), F32), pltpu.VMEM((8 * ROWS, 2 * D), F32)]


def first(notes, q, q_other, parts):
    return pl.pallas_call(
        first_kernel,
        out_shape=(*state_shape(16), jax.ShapeDtypeStruct((16, SPAN, 2 * D), BF16), HAVE_SHAPE),
        in_specs=[VMEM_SPEC] * 4 + [ANY_SPEC] * 2,
        out_specs=(VMEM_SPEC,) * 4,
        scratch_shapes=scratch(32, 16, 2),
        compiler_params=PARAMS,
        cost_estimate=cost(16 * ROWS * 1024),
        name="first",
    )(*notes, q, q_other, *parts)


PAGES = jax.ShapeDtypeStruct((8, SPAN, 2 * D), BF16)


def give(note, q, m, acc, page, parts):
    return pl.pallas_call(
        give_kernel,
        out_shape=(jax.ShapeDtypeStruct((8 * SPAN + META, GROUP * D), BF16), PAGES),
        in_specs=[VMEM_SPEC] * 5 + [ANY_SPEC] * 4,
        out_specs=(VMEM_SPEC,) * 2,
        scratch_shapes=STATE + [pltpu.VMEM((META, GROUP * D), F32)] + scratch(64, 8, 4),
        compiler_params=PARAMS,
        cost_estimate=cost(8 * ROWS * 2048),
        name="give",
    )(note, q, m, acc, page, *parts)


def own(note, q, m, acc, page, have, parts):
    return pl.pallas_call(
        own_kernel,
        out_shape=(*state_shape(8), PAGES, HAVE_SHAPE),
        in_specs=[VMEM_SPEC] * 6 + [ANY_SPEC] * 8,
        out_specs=(VMEM_SPEC,) * 4,
        scratch_shapes=STATE + scratch(128, 8, 8),
        compiler_params=PARAMS,
        cost_estimate=cost(8 * ROWS * 4096),
        name="own",
    )(note, q, m, acc, page, have, *parts)


def merge(m, acc, take, page, found, take_page):
    return pl.pallas_call(
        merge_kernel,
        out_shape=jax.ShapeDtypeStruct((4, 3 * SPAN, GROUP * D), BF16),
        in_specs=[VMEM_SPEC] * 6,
        out_specs=VMEM_SPEC,
        compiler_params=SMALL,
        name="merge",
    )(m, acc, take, page, found, take_page)


def finish(x):
    return pl.pallas_call(
        finish_kernel,
        out_shape=(
            jax.ShapeDtypeStruct((2 * SPAN, HEADS * GROUP * D), BF16),
            jax.ShapeDtypeStruct((2, SPAN, HEADS * D), BF16),
            jax.ShapeDtypeStruct((2, SPAN, HEADS * D), BF16),
        ),
        in_specs=[VMEM_SPEC],
        out_specs=(VMEM_SPEC,) * 3,
        compiler_params=SMALL,
        name="finish",
    )(x)


def local(queries, k, ks, v, vs, span_pos, page_of_slot):
    pack = prep(span_pos, page_of_slot, queries, k, ks, v, vs)
    pack = lax.all_to_all(pack.reshape(HEADS * PACK, 2 * D), "y", 0, 0, tiled=True)
    a, b, q, note = split(pack.reshape(4, PACK, 2 * D))
    q_other, note_other = shift(q, "c", 1), shift(note, "c", 1)
    notes = (note, note_other)

    a1, a2, a3 = shift(a, "z", -1), shift(a, "z", 2), shift(a, "z", 1)
    b1, b2, b3 = shift(b, X, -1), shift(b, X, 2), shift(b, X, 1)
    b3, q_other = lax.optimization_barrier((b3, q_other))
    moves = [(i, 0, i // 4, i % 4 * PIECE, PIECE) for i in range(8)]
    a, b = move("join", moves, (4 * PIECE, 4 * PIECE), a, a1, a2, a3, b, b1, b2, b3)
    a_next, a_prev = shift(a, X, -1), shift(a, X, 1)
    b_next, b_prev = shift(b, "z", -1), shift(b, "z", 1)

    m, acc, page, have = first(notes, q, q_other, (a, b))

    near = (a_next, a_prev, b_next, b_prev)
    near, m, acc, page, have = lax.optimization_barrier((near, m, acc, page, have))
    a_next, a_prev, b_next, b_prev = near
    far = (shift(a_prev, X, 1), shift(b_prev, "z", 1), cross(a_next, X, -1), cross(b_next, "z", -1))

    give_o, give_p = give(note_other, q_other, m, acc, page, near)
    take, take_page = shift(give_o, "c", 1), shift(give_p, "c", 1)
    m, acc, page, found = own(note, q, m, acc, page, have, (*near, *far))
    out = merge(m, acc, take, page, found, take_page)
    out = lax.all_to_all(out.reshape(4 * 3 * SPAN, GROUP * D), "y", 0, 0, tiled=True)
    return finish(out.reshape(4, 3 * SPAN, GROUP * D))


def solution(mesh):
    fine = Mesh(mesh.devices.reshape(2, 4, 2, 4, 2), AXES)
    rows, flat = P(AXES, None), P(AXES)
    return jax.shard_map(
        local,
        mesh=fine,
        in_specs=(rows, rows, rows, rows, rows, flat, flat),
        out_specs=(rows, P(AXES, None, None), P(AXES, None, None)),
        check_vma=False,
    )
```

```python
import functools
import math

import jax
import jax.numpy as jnp
from jax import lax
from jax.experimental import pallas as pl
from jax.experimental.pallas import tpu as pltpu
from jax.sharding import Mesh
from jax.sharding import PartitionSpec as P

AXES = ("xh", "z", "c", "y", "xl")
X = ("xh", "xl")
BF16 = jnp.bfloat16
F32 = jnp.float32
SPAN = 64
HEADS = 4
GROUP = 4
D = 128
ROWS = GROUP * SPAN
PAIR = 2 * ROWS
CHUNK = 64
FACTOR = math.log2(math.e) / math.sqrt(D)
LOW = -1e30
META = 16
PIECE = 4 * SPAN + META
PACK = 2 * SPAN + META + 4 * SPAN
RANK, FULL, TURN, SLOT = range(4)
NT = (((1,), (1,)), ((), ()))
VMEM_SPEC = pl.BlockSpec(memory_space=pltpu.VMEM)
SMEM_SPEC = pl.BlockSpec(memory_space=pltpu.SMEM)
ANY_SPEC = pl.BlockSpec(memory_space=pl.ANY)


SMALL = pltpu.CompilerParams(vmem_limit_bytes=8 * 2**20)
PARAMS = pltpu.CompilerParams(vmem_limit_bytes=24 * 2**20)


def shift(x, axis, by):
    size = 2 if axis == "c" else 4
    return lax.ppermute(x, axis, [(i, (i + by) % size) for i in range(size)])


def cross(x, axis, by):
    if axis == "z":
        axes, at = ("z", "c"), lambda i, c: 2 * i + c
    else:
        axes, at = ("xh", "c", "xl"), lambda i, c: i // 2 * 4 + c * 2 + i % 2
    pairs = [(at(i, c), at((i + by) % 4, 1 - c)) for i in range(4) for c in range(2)]
    return lax.ppermute(x, axes, pairs)


def prep_kernel(pos_ref, slot_ref, q_ref, k_ref, ks_ref, v_ref, vs_ref, out):
    rows = k_ref.shape[0]
    row = lax.broadcasted_iota(jnp.int32, (META, 2 * D), 0)
    meta = jnp.zeros((META, 2 * D), F32)
    for r in range(2):
        meta = jnp.where(row == r, pos_ref[r].astype(F32), meta)
        meta = jnp.where(row == 2 + r, slot_ref[r].astype(F32), meta)
    ks, vs = ks_ref[...].astype(F32).T, vs_ref[...].astype(F32).T
    for h in range(HEADS):
        at = slice(h * D, (h + 1) * D)
        out[h, :rows, :D] = (k_ref[:, at].astype(F32) * ks[:, h : h + 1]).astype(BF16)
        out[h, :rows, D:] = (v_ref[:, at].astype(F32) * vs[:, h : h + 1]).astype(BF16)
        out[h, rows : rows + META, :] = meta.astype(BF16)
        for i in range(2):
            first = rows + META + i * rows
            at = slice((h * 2 + i) * 2 * D, (h * 2 + i + 1) * 2 * D)
            out[h, first : first + rows, :] = q_ref[:, at]


def prep(pos, slot, queries, k, ks, v, vs):
    return pl.pallas_call(
        prep_kernel,
        out_shape=jax.ShapeDtypeStruct((HEADS, PACK, 2 * D), BF16),
        in_specs=[SMEM_SPEC] * 2 + [VMEM_SPEC] * 5,
        out_specs=VMEM_SPEC,
        name="prep",
    )(pos, slot, queries, k, ks.T, v, vs.T)


def split_kernel(x_ref, a_ref, b_ref, q_ref):
    note = jnp.concatenate([x_ref[y, 2 * SPAN : 2 * SPAN + META, :].astype(F32)[:4] for y in range(4)], axis=0)
    note = note.astype(BF16)
    for i, ref in enumerate((a_ref, b_ref)):
        for y in range(4):
            ref[y * SPAN : (y + 1) * SPAN, :] = x_ref[y, i * SPAN : (i + 1) * SPAN, :]
        ref[4 * SPAN :, :] = note
    rows = 2 * SPAN
    for y in range(4):
        for i in range(2):
            first = rows + META + i * rows
            q_ref[y * rows : (y + 1) * rows, i * 2 * D : (i + 1) * 2 * D] = x_ref[y, first : first + rows, :]
            q_ref[4 * rows :, i * 2 * D : (i + 1) * 2 * D] = note


def split(x):
    return pl.pallas_call(
        split_kernel,
        out_shape=(
            jax.ShapeDtypeStruct((PIECE, 2 * D), BF16),
            jax.ShapeDtypeStruct((PIECE, 2 * D), BF16),
            jax.ShapeDtypeStruct((8 * SPAN + META, GROUP * D), BF16),
        ),
        in_specs=[VMEM_SPEC],
        out_specs=(VMEM_SPEC,) * 3,
        compiler_params=SMALL,
        name="split",
    )(x)


def copy_kernel(moves, inputs, *refs):
    ins, rest = refs[:inputs], refs[inputs:]
    outs, sem = rest[:-1], rest[-1]
    copies = [
        pltpu.make_async_copy(ins[i].at[pl.ds(a, n), :], outs[o].at[pl.ds(b, n), :], sem.at[c])
        for c, (i, a, o, b, n) in enumerate(moves)
    ]
    for copy in copies:
        copy.start()
    for copy in copies:
        copy.wait()


def move(name, moves, rows, *arrays):
    return pl.pallas_call(
        functools.partial(copy_kernel, moves, len(arrays)),
        out_shape=tuple(jax.ShapeDtypeStruct((r, 2 * D), BF16) for r in rows),
        in_specs=[ANY_SPEC] * len(arrays),
        out_specs=(VMEM_SPEC,) * len(rows),
        scratch_shapes=[pltpu.SemaphoreType.DMA((len(moves),))],
        compiler_params=SMALL,
        name=name,
    )(*arrays)


def offsets(pieces):
    return [p * PIECE + y * SPAN for p in range(pieces) for y in range(4)]


def load_parts(parts, kv_s, sem):
    copies, row = [], 0
    for i, part in enumerate(parts):
        copies.append(pltpu.make_async_copy(part, kv_s.at[pl.ds(row, part.shape[0]), :], sem.at[i]))
        row += part.shape[0]
    for copy in copies:
        copy.start()
    return copies


def tables(kinds, kv_s, q_refs, tab_v, tab, sem):
    count = len(kinds) * 4
    row = lax.broadcasted_iota(jnp.int32, (META, D), 0)
    lane = lax.broadcasted_iota(jnp.int32, (META, D), 1)
    place = jnp.zeros((1, D), F32)
    for p, kind in enumerate(kinds):
        x = kv_s[p * PIECE + 4 * SPAN : (p + 1) * PIECE, :D].astype(F32)
        hit = jnp.logical_and(row == (lane - p * 4) * 4 + kind, jnp.logical_and(lane >= p * 4, lane < p * 4 + 4))
        place = place + jnp.sum(jnp.where(hit, x, 0.0), axis=0, keepdims=True)
    q_place, slot = jnp.zeros((1, D), F32), jnp.zeros((1, D), F32)
    for half, ref in enumerate(q_refs):
        x = ref[8 * SPAN :, :D].astype(F32)
        j = lane - half * 8
        hit = jnp.logical_and(jnp.logical_and(j >= 0, j < 8), row == (j // 2) * 4 + j % 2)
        q_place = q_place + jnp.sum(jnp.where(hit, x, 0.0), axis=0, keepdims=True)
        hit = jnp.logical_and(jnp.logical_and(j >= 0, j < 8), row == (j // 2) * 4 + j % 2 + 2)
        slot = slot + jnp.sum(jnp.where(hit, x, 0.0), axis=0, keepdims=True)
    big_row = lax.broadcasted_iota(jnp.int32, (D, D), 0)
    down = jnp.broadcast_to(place, (D, D)).T
    inside = big_row < count

    def below(x, limit, where):
        return jnp.sum(jnp.where(jnp.logical_and(x < limit, where), 1.0, 0.0), axis=0, keepdims=True).astype(jnp.int32)

    tab_v[RANK : RANK + 1, :] = below(down, place, inside)
    tab_v[FULL : FULL + 1, :] = below(down, q_place, inside)
    q_down = jnp.broadcast_to(q_place, (D, D)).T
    big_lane = lax.broadcasted_iota(jnp.int32, (D, D), 1)
    same = jnp.logical_and(big_row // 8 == big_lane // 8, big_row < 8 * len(q_refs))
    tab_v[TURN : TURN + 1, :] = below(q_down, q_place, same) + lane[:1] // 8 * 8
    at = ((big_row // 4) * PIECE + big_row % 4 * SPAN + 1).astype(F32)
    hit = jnp.logical_and(down == slot, inside)
    tab_v[SLOT : SLOT + 1, :] = jnp.sum(jnp.where(hit, at, 0.0), axis=0, keepdims=True).astype(jnp.int32) - 1
    copy = pltpu.make_async_copy(tab_v, tab, sem)
    copy.start()
    copy.wait()


def place_queries(q_refs, tab, q_s):
    for half, q_ref in enumerate(q_refs):
        for j in range(8):
            first = tab[TURN, half * 8 + j] * ROWS
            for g in range(GROUP):
                at = pl.ds(pl.multiple_of(first + g * SPAN, SPAN), SPAN)
                q_s[at, :] = q_ref[j * SPAN : (j + 1) * SPAN, g * D : (g + 1) * D]


def flash(spans, count, diagonal, tab, q_s, kv_s, m_s, acc, work):
    s_a, s_b, p_a, p_b, al_a, al_b, hot, order, full_s, own_s, *lists = work
    block = s_a.shape[1]
    sizes = [block // SPAN >> i for i in range(len(lists))]
    least = sizes[-1]
    for i, row in enumerate(offsets(spans // 4)):
        order[tab[RANK, i]] = row
    for j in range(count):
        full_s[tab[TURN, j]] = tab[FULL, j]
        own_s[tab[TURN, j]] = 1 if diagonal and j < 8 else 0
    if not diagonal:
        key = lax.broadcasted_iota(jnp.int32, (block, D), 0)
        hot[...] = jnp.where(lax.broadcasted_iota(jnp.int32, (block, D), 1) == key // SPAN, 1.0, 0.0).astype(BF16)

    counts = [jnp.int32(0)] * len(lists)
    for pair in range(count // 2):
        seen = jnp.maximum(full_s[2 * pair] + own_s[2 * pair], full_s[2 * pair + 1] + own_s[2 * pair + 1])
        seen = lax.div(seen + least - 1, least) * least
        at = jnp.int32(0)
        for i, (items, per) in enumerate(zip(lists, sizes)):
            some = lax.div(seen - at, per)

            def put(b, _, items=items, per=per, pair=pair, first=counts[i], at=at):
                items[0, first + b] = pair
                items[1, first + b] = jnp.minimum(at + b * per, spans - per)
                items[2, first + b] = at + b * per
                return 0

            lax.fori_loop(0, some, put, 0)
            counts[i] = counts[i] + some
            at = at + some * per
    for items, n in zip(lists, counts):
        for extra in range(3):
            items[0, n + extra] = 0
            items[1, n + extra] = 0
            items[2, n + extra] = 1 << 20

    def sweep(size, items, total):
        per, cols = size // SPAN, slice(0, size)

        def rows_of(t):
            return pl.ds(pl.multiple_of(items[0, t] * PAIR, PAIR), PAIR)

        def keys_of(t, lanes):
            first = items[1, t]
            return jnp.concatenate(
                [kv_s[pl.ds(pl.multiple_of(order[first + i], 16), SPAN), lanes] for i in range(per)], axis=0
            )

        def scores(t, s):
            q, k = q_s[rows_of(t), :], keys_of(t, slice(0, D))
            if not diagonal:
                lane = lax.broadcasted_iota(jnp.int32, (ROWS, D), 1)
                shut = [
                    jnp.where(lane < full_s[items[0, t] * 2 + i] - items[2, t], 0.0, LOW).astype(BF16)
                    for i in range(2)
                ]
                q = jnp.concatenate([q, jnp.concatenate(shut, axis=0)], axis=1)
                k = jnp.concatenate([k, hot[cols, :]], axis=1)
            s[:, cols] = lax.dot_general(q, k, NT, preferred_element_type=F32)

        def weigh(t, s, p, al):
            first = pl.multiple_of(items[0, t] * PAIR, PAIR)
            token = lax.broadcasted_iota(jnp.int32, (CHUNK, D), 0) + 1
            lane = lax.broadcasted_iota(jnp.int32, (CHUNK, D), 1)
            for c in range(PAIR // CHUNK):
                r = slice(c * CHUNK, (c + 1) * CHUNK)
                tiles = [s[r, u * D : (u + 1) * D] for u in range(size // D)]
                if diagonal:
                    which = items[0, t] * 2 + c * CHUNK // ROWS
                    limit = (full_s[which] - items[2, t]) * SPAN + own_s[which] * (token + (c * CHUNK) % SPAN)
                    gap = lane - limit
                    tiles = [jnp.where(gap < -u * D, x, LOW) for u, x in enumerate(tiles)]
                top = functools.reduce(jnp.maximum, tiles)
                top = jnp.broadcast_to(jnp.max(top, axis=1, keepdims=True), (CHUNK, D)) * FACTOR
                at = pl.ds(first + c * CHUNK, CHUNK)
                old = m_s[at, :]
                new = jnp.maximum(old, top)
                m_s[at, :] = new
                al[r, :] = jnp.exp2(old - new)
                for u, x in enumerate(tiles):
                    p[r, u * D : (u + 1) * D] = jnp.exp2(x * FACTOR - new).astype(BF16)

        def gather(t, p, al_ref):
            v = keys_of(t, slice(D, 2 * D))
            v = jnp.concatenate([v, jnp.ones((size, D), BF16)], axis=1)
            o = lax.dot(p[:, cols], v, preferred_element_type=F32)
            al = al_ref[...]
            rows = rows_of(t)
            acc[rows, :] = acc[rows, :] * jnp.concatenate([al, al], axis=1) + o

        scores(0, s_a)

        def body(i, _):
            t = 2 * i
            scores(t + 1, s_b)
            weigh(t, s_a, p_a, al_a)
            gather(t, p_a, al_a)
            scores(t + 2, s_a)
            weigh(t + 1, s_b, p_b, al_b)
            gather(t + 1, p_b, al_b)
            return 0

        lax.fori_loop(0, (total + 1) // 2, body, 0)

    for items, per, n in zip(lists, sizes, counts):
        sweep(per * SPAN, items, n)


def work_shapes(spans, count, block, levels):
    return [
        pltpu.VMEM((PAIR, block), F32),
        pltpu.VMEM((PAIR, block), F32),
        pltpu.VMEM((PAIR, block), BF16),
        pltpu.VMEM((PAIR, block), BF16),
        pltpu.VMEM((PAIR, D), F32),
        pltpu.VMEM((PAIR, D), F32),
        pltpu.VMEM((block, D), BF16),
        pltpu.SMEM((spans + 32,), jnp.int32),
        pltpu.SMEM((count,), jnp.int32),
        pltpu.SMEM((count,), jnp.int32),
    ] + [pltpu.SMEM((3, count // 2 * (spans * SPAN // (block >> i)) + 8), jnp.int32) for i in range(levels)]


def scratch(spans, count, parts, block=1024, levels=2):
    return [
        pltpu.VMEM((spans // 4 * PIECE, 2 * D), BF16),
        pltpu.VMEM((count * ROWS, D), BF16),
        pltpu.SemaphoreType.DMA((parts,)),
        pltpu.VMEM((8, D), jnp.int32),
        pltpu.SMEM((8, D), jnp.int32),
        pltpu.SemaphoreType.DMA,
    ] + work_shapes(spans, count, block, levels)


def chunk_row(tab, j):
    return pl.ds(pl.multiple_of(jnp.maximum(tab[SLOT, j], 0), 16), SPAN)


def first_kernel(qa_ref, qb_ref, *refs):
    parts, (m_s, acc, page, have), rest = refs[:2], refs[2:6], refs[6:]
    kv_s, q_s, sem, tab_v, tab, tab_sem, *work = rest
    copies = load_parts(parts, kv_s, sem)
    m_s[...] = jnp.full(m_s.shape, LOW, F32)
    acc[...] = jnp.zeros(acc.shape, F32)
    for copy in copies:
        copy.wait()
    tables((0,) * 4 + (1,) * 4, kv_s, (qa_ref, qb_ref), tab_v, tab, tab_sem)
    have[...] = tab_v[SLOT : SLOT + 1, :]
    for j in range(16):
        page[j] = kv_s[chunk_row(tab, j), :]
    place_queries((qa_ref, qb_ref), tab, q_s)
    flash(32, 16, True, tab, q_s, kv_s, m_s, acc, work)


def give_kernel(q_ref, m_in, acc_in, page_in, *refs):
    parts, (give_o, give_p), rest = refs[:4], refs[4:6], refs[6:]
    m_s, acc, levels_s, kv_s, q_s, sem, tab_v, tab, tab_sem, *work = rest
    copies = load_parts(parts, kv_s, sem)
    levels_s[...] = jnp.zeros(levels_s.shape, F32)
    m_s[...] = m_in[8 * ROWS :, :]
    acc[...] = acc_in[8 * ROWS :, :]
    for copy in copies:
        copy.wait()
    tables((0,) * 8 + (1,) * 8, kv_s, (q_ref,), tab_v, tab, tab_sem)
    for j in range(8):
        near = kv_s[chunk_row(tab, j), :].astype(F32)
        give_p[j] = jnp.where(tab[SLOT, j] >= 0, near, page_in[8 + j].astype(F32)).astype(BF16)
    place_queries((q_ref,), tab, q_s)
    flash(64, 8, False, tab, q_s, kv_s, m_s, acc, work)
    for g in range(GROUP):
        for block in range(4):
            logs = []
            for j in (2 * block, 2 * block + 1):
                rows = pl.ds(pl.multiple_of(tab[TURN, j] * ROWS + g * SPAN, SPAN), SPAN)
                sums = jnp.maximum(acc[rows, D:], 1e-30)
                give_o[j * SPAN : (j + 1) * SPAN, g * D : (g + 1) * D] = (acc[rows, :D] * (1.0 / sums)).astype(BF16)
                logs.append(m_s[rows, :] + jnp.log(sums) * math.log2(math.e))
            level = jnp.concatenate(logs, axis=0).T[:1, :]
            for part in range(3):
                piece = level.astype(BF16).astype(F32)
                level = level - piece
                levels_s[part * 4 + g : part * 4 + g + 1, block * D : (block + 1) * D] = piece
    give_o[8 * SPAN :, :] = levels_s[...].astype(BF16)


def own_kernel(q_ref, m_in, acc_in, page_in, have, *refs):
    parts, (m_out, acc_out, page, found), rest = refs[:8], refs[8:12], refs[12:]
    m_s, acc, kv_s, q_s, sem, tab_v, tab, tab_sem, *work = rest
    copies = load_parts(parts, kv_s, sem)
    m_s[...] = m_in[: 8 * ROWS, :]
    acc[...] = acc_in[: 8 * ROWS, :]
    for copy in copies:
        copy.wait()
    tables((0,) * 8 + (1,) * 8 + ((0,) * 4 + (1,) * 4) * 2, kv_s, (q_ref,), tab_v, tab, tab_sem)
    found[...] = jnp.maximum(have[...], tab_v[SLOT : SLOT + 1, :])
    for j in range(8):
        near = kv_s[chunk_row(tab, j), :].astype(F32)
        page[j] = jnp.where(tab[SLOT, j] >= 0, near, page_in[j].astype(F32)).astype(BF16)
    place_queries((q_ref,), tab, q_s)
    flash(128, 8, False, tab, q_s, kv_s, m_s, acc, work)
    for j in range(8):
        rows = pl.ds(pl.multiple_of(tab[TURN, j] * ROWS, ROWS), ROWS)
        m_out[j * ROWS : (j + 1) * ROWS, :] = m_s[rows, :]
        acc_out[j * ROWS : (j + 1) * ROWS, :] = acc[rows, :]


def merge_kernel(m_in, acc_in, take, page, found, take_p, out):
    levels = take[8 * SPAN :, :].astype(F32)
    for g in range(GROUP):
        level = levels[g : g + 1] + levels[4 + g : 5 + g] + levels[8 + g : 9 + g]
        for block in range(4):
            both = jnp.broadcast_to(level[:, block * D : (block + 1) * D], (D, D)).T
            for j in (2 * block, 2 * block + 1):
                y, ab = divmod(j, 2)
                rows = slice(j * ROWS + g * SPAN, j * ROWS + (g + 1) * SPAN)
                m_a, m_b = m_in[rows, :], both[j % 2 * SPAN : (j % 2 + 1) * SPAN]
                top = jnp.maximum(m_a, m_b)
                w_a, w_b = jnp.exp2(m_a - top), jnp.exp2(m_b - top)
                o_b = take[j * SPAN : (j + 1) * SPAN, g * D : (g + 1) * D].astype(F32)
                total = acc_in[rows, D:] * w_a + w_b
                o = (acc_in[rows, :D] * w_a + o_b * w_b) * (1.0 / total)
                out[y, ab * SPAN : (ab + 1) * SPAN, g * D : (g + 1) * D] = o.astype(BF16)
    lane = lax.broadcasted_iota(jnp.int32, (1, D), 1)
    for j in range(8):
        y, s = divmod(j, 2)
        here = jnp.max(jnp.where(lane == j, found[...], -1), axis=1, keepdims=True) >= 0
        x = jnp.where(here, page[j].astype(F32), take_p[j].astype(F32))
        out[y, 2 * SPAN :, s * 2 * D : (s + 1) * 2 * D] = x.astype(BF16)


def finish_kernel(x_ref, o_ref, k_ref, v_ref):
    for h in range(HEADS):
        o_ref[:, h * GROUP * D : (h + 1) * GROUP * D] = x_ref[h, : 2 * SPAN, :]
        for s in range(2):
            at = 2 * s * D
            k_ref[s, :, h * D : (h + 1) * D] = x_ref[h, 2 * SPAN :, at : at + D]
            v_ref[s, :, h * D : (h + 1) * D] = x_ref[h, 2 * SPAN :, at + D : at + 2 * D]


def cost(scores):
    return pl.CostEstimate(flops=scores * 2048, bytes_accessed=2**20, transcendentals=0)


HAVE_SHAPE = jax.ShapeDtypeStruct((1, D), jnp.int32)


def state_shape(count):
    return [jax.ShapeDtypeStruct((count * ROWS, D), F32), jax.ShapeDtypeStruct((count * ROWS, 2 * D), F32)]


STATE = [pltpu.VMEM((8 * ROWS, D), F32), pltpu.VMEM((8 * ROWS, 2 * D), F32)]


def first(q, q_other, parts):
    return pl.pallas_call(
        first_kernel,
        out_shape=(*state_shape(16), jax.ShapeDtypeStruct((16, SPAN, 2 * D), BF16), HAVE_SHAPE),
        in_specs=[VMEM_SPEC] * 2 + [ANY_SPEC] * 2,
        out_specs=(VMEM_SPEC,) * 4,
        scratch_shapes=scratch(32, 16, 2),
        compiler_params=PARAMS,
        cost_estimate=cost(16 * ROWS * 1024),
        name="first",
    )(q, q_other, *parts)


PAGES = jax.ShapeDtypeStruct((8, SPAN, 2 * D), BF16)


def give(q, m, acc, page, parts):
    return pl.pallas_call(
        give_kernel,
        out_shape=(jax.ShapeDtypeStruct((8 * SPAN + META, GROUP * D), BF16), PAGES),
        in_specs=[VMEM_SPEC] * 4 + [ANY_SPEC] * 4,
        out_specs=(VMEM_SPEC,) * 2,
        scratch_shapes=STATE + [pltpu.VMEM((META, GROUP * D), F32)] + scratch(64, 8, 4),
        compiler_params=PARAMS,
        cost_estimate=cost(8 * ROWS * 2048),
        name="give",
    )(q, m, acc, page, *parts)


def own(q, m, acc, page, have, parts):
    return pl.pallas_call(
        own_kernel,
        out_shape=(*state_shape(8), PAGES, HAVE_SHAPE),
        in_specs=[VMEM_SPEC] * 5 + [ANY_SPEC] * 8,
        out_specs=(VMEM_SPEC,) * 4,
        scratch_shapes=STATE + scratch(128, 8, 8),
        compiler_params=PARAMS,
        cost_estimate=cost(8 * ROWS * 4096),
        name="own",
    )(q, m, acc, page, have, *parts)


def merge(m, acc, take, page, found, take_page):
    return pl.pallas_call(
        merge_kernel,
        out_shape=jax.ShapeDtypeStruct((4, 3 * SPAN, GROUP * D), BF16),
        in_specs=[VMEM_SPEC] * 6,
        out_specs=VMEM_SPEC,
        compiler_params=SMALL,
        name="merge",
    )(m, acc, take, page, found, take_page)


def finish(x):
    return pl.pallas_call(
        finish_kernel,
        out_shape=(
            jax.ShapeDtypeStruct((2 * SPAN, HEADS * GROUP * D), BF16),
            jax.ShapeDtypeStruct((2, SPAN, HEADS * D), BF16),
            jax.ShapeDtypeStruct((2, SPAN, HEADS * D), BF16),
        ),
        in_specs=[VMEM_SPEC],
        out_specs=(VMEM_SPEC,) * 3,
        compiler_params=SMALL,
        name="finish",
    )(x)


def local(queries, k, ks, v, vs, span_pos, page_of_slot):
    pack = prep(span_pos, page_of_slot, queries, k, ks, v, vs)
    pack = lax.all_to_all(pack.reshape(HEADS * PACK, 2 * D), "y", 0, 0, tiled=True)
    a, b, q = split(pack.reshape(4, PACK, 2 * D))

    a1, a2, a3 = shift(a, "z", -1), shift(a, "z", 2), shift(a, "z", 1)
    b1, b2, b3 = shift(b, X, -1), shift(b, X, 2), shift(b, X, 1)
    a1, a2, a3, b1, b2, b3, q = lax.optimization_barrier((a1, a2, a3, b1, b2, b3, q))
    q_other = shift(q, "c", 1)
    moves = [(i, 0, i // 4, i % 4 * PIECE, PIECE) for i in range(8)]
    a, b = move("join", moves, (4 * PIECE, 4 * PIECE), a, a1, a2, a3, b, b1, b2, b3)
    a_next, a_prev = shift(a, X, -1), shift(a, X, 1)
    b_next, b_prev = shift(b, "z", -1), shift(b, "z", 1)

    m, acc, page, have = first(q, q_other, (a, b))

    near = (a_next, a_prev, b_next, b_prev)
    near, m, acc, page, have = lax.optimization_barrier((near, m, acc, page, have))
    a_next, a_prev, b_next, b_prev = near
    far = (shift(a_prev, X, 1), shift(b_prev, "z", 1), cross(a_next, X, -1), cross(b_next, "z", -1))

    give_o, give_p = give(q_other, m, acc, page, near)
    take, take_page = shift(give_o, "c", 1), shift(give_p, "c", 1)
    m, acc, page, found = own(q, m, acc, page, have, (*near, *far))
    out = merge(m, acc, take, page, found, take_page)
    out = lax.all_to_all(out.reshape(4 * 3 * SPAN, GROUP * D), "y", 0, 0, tiled=True)
    return finish(out.reshape(4, 3 * SPAN, GROUP * D))


def solution(mesh):
    fine = Mesh(mesh.devices.reshape(2, 4, 2, 4, 2), AXES)
    rows, flat = P(AXES, None), P(AXES)
    return jax.shard_map(
        local,
        mesh=fine,
        in_specs=(rows, rows, rows, rows, rows, flat, flat),
        out_specs=(rows, P(AXES, None, None), P(AXES, None, None)),
        check_vma=False,
    )
```

```python
import functools
import math

import jax
import jax.numpy as jnp
from jax import lax
from jax.experimental import pallas as pl
from jax.experimental.pallas import tpu as pltpu
from jax.sharding import Mesh
from jax.sharding import PartitionSpec as P

AXES = ("xh", "z", "c", "y", "xl")
X = ("xh", "xl")
BF16 = jnp.bfloat16
F32 = jnp.float32
SPAN = 64
HEADS = 4
GROUP = 4
D = 128
ROWS = GROUP * SPAN
PAIR = 2 * ROWS
CHUNK = 64
FACTOR = math.log2(math.e) / math.sqrt(D)
LOW = -1e30
META = 16
PIECE = 4 * SPAN + META
PACK = 2 * SPAN + META + 4 * SPAN
RANK, FULL, TURN, SLOT = range(4)
NT = (((1,), (1,)), ((), ()))
VMEM_SPEC = pl.BlockSpec(memory_space=pltpu.VMEM)
SMEM_SPEC = pl.BlockSpec(memory_space=pltpu.SMEM)
ANY_SPEC = pl.BlockSpec(memory_space=pl.ANY)


SMALL = pltpu.CompilerParams(vmem_limit_bytes=8 * 2**20)
PARAMS = pltpu.CompilerParams(vmem_limit_bytes=24 * 2**20)


def shift(x, axis, by):
    size = 2 if axis == "c" else 4
    return lax.ppermute(x, axis, [(i, (i + by) % size) for i in range(size)])


def cross(x, axis, by):
    if axis == "z":
        axes, at = ("z", "c"), lambda i, c: 2 * i + c
    else:
        axes, at = ("xh", "c", "xl"), lambda i, c: i // 2 * 4 + c * 2 + i % 2
    pairs = [(at(i, c), at((i + by) % 4, 1 - c)) for i in range(4) for c in range(2)]
    return lax.ppermute(x, axes, pairs)


def prep_kernel(pos_ref, slot_ref, q_ref, k_ref, ks_ref, v_ref, vs_ref, out):
    rows = k_ref.shape[0]
    row = lax.broadcasted_iota(jnp.int32, (META, 2 * D), 0)
    meta = jnp.zeros((META, 2 * D), F32)
    for r in range(2):
        meta = jnp.where(row == r, pos_ref[r].astype(F32), meta)
        meta = jnp.where(row == 2 + r, slot_ref[r].astype(F32), meta)
    ks, vs = ks_ref[...].astype(F32).T, vs_ref[...].astype(F32).T
    for h in range(HEADS):
        at = slice(h * D, (h + 1) * D)
        out[h, :rows, :D] = (k_ref[:, at].astype(F32) * ks[:, h : h + 1]).astype(BF16)
        out[h, :rows, D:] = (v_ref[:, at].astype(F32) * vs[:, h : h + 1]).astype(BF16)
        out[h, rows : rows + META, :] = meta.astype(BF16)
        for i in range(2):
            first = rows + META + i * rows
            at = slice((h * 2 + i) * 2 * D, (h * 2 + i + 1) * 2 * D)
            out[h, first : first + rows, :] = q_ref[:, at]


def prep(pos, slot, queries, k, ks, v, vs):
    return pl.pallas_call(
        prep_kernel,
        out_shape=jax.ShapeDtypeStruct((HEADS, PACK, 2 * D), BF16),
        in_specs=[SMEM_SPEC] * 2 + [VMEM_SPEC] * 5,
        out_specs=VMEM_SPEC,
        name="prep",
    )(pos, slot, queries, k, ks.T, v, vs.T)


def split_kernel(x_ref, a_ref, b_ref, q_ref):
    note = jnp.concatenate([x_ref[y, 2 * SPAN : 2 * SPAN + META, :].astype(F32)[:4] for y in range(4)], axis=0)
    note = note.astype(BF16)
    for i, ref in enumerate((a_ref, b_ref)):
        for y in range(4):
            ref[y * SPAN : (y + 1) * SPAN, :] = x_ref[y, i * SPAN : (i + 1) * SPAN, :]
        ref[4 * SPAN :, :] = note
    rows = 2 * SPAN
    for y in range(4):
        for i in range(2):
            first = rows + META + i * rows
            q_ref[y * rows : (y + 1) * rows, i * 2 * D : (i + 1) * 2 * D] = x_ref[y, first : first + rows, :]
            q_ref[4 * rows :, i * 2 * D : (i + 1) * 2 * D] = note


def split(x):
    return pl.pallas_call(
        split_kernel,
        out_shape=(
            jax.ShapeDtypeStruct((PIECE, 2 * D), BF16),
            jax.ShapeDtypeStruct((PIECE, 2 * D), BF16),
            jax.ShapeDtypeStruct((8 * SPAN + META, GROUP * D), BF16),
        ),
        in_specs=[VMEM_SPEC],
        out_specs=(VMEM_SPEC,) * 3,
        compiler_params=SMALL,
        name="split",
    )(x)


def join_kernel(*refs):
    for i, ref in enumerate(refs[:8]):
        refs[8 + i // 4][i % 4 * PIECE : (i % 4 + 1) * PIECE, :] = ref[...]


def join(*pieces):
    return pl.pallas_call(
        join_kernel,
        out_shape=(jax.ShapeDtypeStruct((4 * PIECE, 2 * D), BF16),) * 2,
        in_specs=[VMEM_SPEC] * 8,
        out_specs=(VMEM_SPEC,) * 2,
        compiler_params=SMALL,
        name="join",
    )(*pieces)


def offsets(pieces):
    return [p * PIECE + y * SPAN for p in range(pieces) for y in range(4)]


def load_parts(parts, kv_s, sem):
    copies, row = [], 0
    for i, part in enumerate(parts):
        copies.append(pltpu.make_async_copy(part, kv_s.at[pl.ds(row, part.shape[0]), :], sem.at[i]))
        row += part.shape[0]
    for copy in copies:
        copy.start()
    return copies


def tables(kinds, kv_s, q_refs, tab_v, tab, sem):
    count = len(kinds) * 4
    row = lax.broadcasted_iota(jnp.int32, (META, D), 0)
    lane = lax.broadcasted_iota(jnp.int32, (META, D), 1)
    place = jnp.zeros((1, D), F32)
    for p, kind in enumerate(kinds):
        x = kv_s[p * PIECE + 4 * SPAN : (p + 1) * PIECE, :D].astype(F32)
        hit = jnp.logical_and(row == (lane - p * 4) * 4 + kind, jnp.logical_and(lane >= p * 4, lane < p * 4 + 4))
        place = place + jnp.sum(jnp.where(hit, x, 0.0), axis=0, keepdims=True)
    q_place, slot = jnp.zeros((1, D), F32), jnp.zeros((1, D), F32)
    for half, ref in enumerate(q_refs):
        x = ref[8 * SPAN :, :D].astype(F32)
        j = lane - half * 8
        hit = jnp.logical_and(jnp.logical_and(j >= 0, j < 8), row == (j // 2) * 4 + j % 2)
        q_place = q_place + jnp.sum(jnp.where(hit, x, 0.0), axis=0, keepdims=True)
        hit = jnp.logical_and(jnp.logical_and(j >= 0, j < 8), row == (j // 2) * 4 + j % 2 + 2)
        slot = slot + jnp.sum(jnp.where(hit, x, 0.0), axis=0, keepdims=True)
    big_row = lax.broadcasted_iota(jnp.int32, (D, D), 0)
    down = jnp.broadcast_to(place, (D, D)).T
    inside = big_row < count

    def below(x, limit, where):
        return jnp.sum(jnp.where(jnp.logical_and(x < limit, where), 1.0, 0.0), axis=0, keepdims=True).astype(jnp.int32)

    tab_v[RANK : RANK + 1, :] = below(down, place, inside)
    tab_v[FULL : FULL + 1, :] = below(down, q_place, inside)
    q_down = jnp.broadcast_to(q_place, (D, D)).T
    big_lane = lax.broadcasted_iota(jnp.int32, (D, D), 1)
    same = jnp.logical_and(big_row // 8 == big_lane // 8, big_row < 8 * len(q_refs))
    tab_v[TURN : TURN + 1, :] = below(q_down, q_place, same) + lane[:1] // 8 * 8
    at = ((big_row // 4) * PIECE + big_row % 4 * SPAN + 1).astype(F32)
    hit = jnp.logical_and(down == slot, inside)
    tab_v[SLOT : SLOT + 1, :] = jnp.sum(jnp.where(hit, at, 0.0), axis=0, keepdims=True).astype(jnp.int32) - 1
    copy = pltpu.make_async_copy(tab_v, tab, sem)
    copy.start()
    copy.wait()


def place_queries(q_refs, tab, q_s):
    for half, q_ref in enumerate(q_refs):
        for j in range(8):
            first = tab[TURN, half * 8 + j] * ROWS
            for g in range(GROUP):
                at = pl.ds(pl.multiple_of(first + g * SPAN, SPAN), SPAN)
                q_s[at, :] = q_ref[j * SPAN : (j + 1) * SPAN, g * D : (g + 1) * D]


def flash(spans, count, diagonal, tab, q_s, kv_s, m_s, acc, work):
    s_a, s_b, p_a, p_b, al_a, al_b, hot, order, full_s, own_s, *lists = work
    block = s_a.shape[1]
    sizes = [block // SPAN >> i for i in range(len(lists))]
    least = sizes[-1]
    for i, row in enumerate(offsets(spans // 4)):
        order[tab[RANK, i]] = row
    for j in range(count):
        full_s[tab[TURN, j]] = tab[FULL, j]
        own_s[tab[TURN, j]] = 1 if diagonal and j < 8 else 0
    if not diagonal:
        key = lax.broadcasted_iota(jnp.int32, (block, D), 0)
        hot[...] = jnp.where(lax.broadcasted_iota(jnp.int32, (block, D), 1) == key // SPAN, 1.0, 0.0).astype(BF16)

    counts = [jnp.int32(0)] * len(lists)
    for pair in range(count // 2):
        seen = jnp.maximum(full_s[2 * pair] + own_s[2 * pair], full_s[2 * pair + 1] + own_s[2 * pair + 1])
        seen = lax.div(seen + least - 1, least) * least
        at = jnp.int32(0)
        for i, (items, per) in enumerate(zip(lists, sizes)):
            some = lax.div(seen - at, per)

            def put(b, _, items=items, per=per, pair=pair, first=counts[i], at=at):
                items[0, first + b] = pair
                items[1, first + b] = jnp.minimum(at + b * per, spans - per)
                items[2, first + b] = at + b * per
                return 0

            lax.fori_loop(0, some, put, 0)
            counts[i] = counts[i] + some
            at = at + some * per
    for items, n in zip(lists, counts):
        for extra in range(3):
            items[0, n + extra] = 0
            items[1, n + extra] = 0
            items[2, n + extra] = 1 << 20

    def sweep(size, items, total):
        per, cols = size // SPAN, slice(0, size)

        def rows_of(t):
            return pl.ds(pl.multiple_of(items[0, t] * PAIR, PAIR), PAIR)

        def keys_of(t, lanes):
            first = items[1, t]
            return jnp.concatenate(
                [kv_s[pl.ds(pl.multiple_of(order[first + i], 16), SPAN), lanes] for i in range(per)], axis=0
            )

        def scores(t, s):
            q, k = q_s[rows_of(t), :], keys_of(t, slice(0, D))
            if not diagonal:
                lane = lax.broadcasted_iota(jnp.int32, (ROWS, D), 1)
                shut = [
                    jnp.where(lane < full_s[items[0, t] * 2 + i] - items[2, t], 0.0, LOW).astype(BF16)
                    for i in range(2)
                ]
                q = jnp.concatenate([q, jnp.concatenate(shut, axis=0)], axis=1)
                k = jnp.concatenate([k, hot[cols, :]], axis=1)
            s[:, cols] = lax.dot_general(q, k, NT, preferred_element_type=F32)

        def weigh(t, s, p, al):
            first = pl.multiple_of(items[0, t] * PAIR, PAIR)
            token = lax.broadcasted_iota(jnp.int32, (CHUNK, D), 0) + 1
            lane = lax.broadcasted_iota(jnp.int32, (CHUNK, D), 1)
            for c in range(PAIR // CHUNK):
                r = slice(c * CHUNK, (c + 1) * CHUNK)
                tiles = [s[r, u * D : (u + 1) * D] for u in range(size // D)]
                if diagonal:
                    which = items[0, t] * 2 + c * CHUNK // ROWS
                    limit = (full_s[which] - items[2, t]) * SPAN + own_s[which] * (token + (c * CHUNK) % SPAN)
                    gap = lane - limit
                    tiles = [jnp.where(gap < -u * D, x, LOW) for u, x in enumerate(tiles)]
                top = functools.reduce(jnp.maximum, tiles)
                top = jnp.broadcast_to(jnp.max(top, axis=1, keepdims=True), (CHUNK, D)) * FACTOR
                at = pl.ds(first + c * CHUNK, CHUNK)
                old = m_s[at, :]
                new = jnp.maximum(old, top)
                m_s[at, :] = new
                al[r, :] = jnp.exp2(old - new)
                for u, x in enumerate(tiles):
                    p[r, u * D : (u + 1) * D] = jnp.exp2(x * FACTOR - new).astype(BF16)

        def gather(t, p, al_ref):
            v = keys_of(t, slice(D, 2 * D))
            v = jnp.concatenate([v, jnp.ones((size, D), BF16)], axis=1)
            o = lax.dot(p[:, cols], v, preferred_element_type=F32)
            al = al_ref[...]
            rows = rows_of(t)
            acc[rows, :] = acc[rows, :] * jnp.concatenate([al, al], axis=1) + o

        scores(0, s_a)

        def body(i, _):
            t = 2 * i
            scores(t + 1, s_b)
            weigh(t, s_a, p_a, al_a)
            gather(t, p_a, al_a)
            scores(t + 2, s_a)
            weigh(t + 1, s_b, p_b, al_b)
            gather(t + 1, p_b, al_b)
            return 0

        lax.fori_loop(0, (total + 1) // 2, body, 0)

    for items, per, n in zip(lists, sizes, counts):
        sweep(per * SPAN, items, n)


def work_shapes(spans, count, block, levels):
    return [
        pltpu.VMEM((PAIR, block), F32),
        pltpu.VMEM((PAIR, block), F32),
        pltpu.VMEM((PAIR, block), BF16),
        pltpu.VMEM((PAIR, block), BF16),
        pltpu.VMEM((PAIR, D), F32),
        pltpu.VMEM((PAIR, D), F32),
        pltpu.VMEM((block, D), BF16),
        pltpu.SMEM((spans + 32,), jnp.int32),
        pltpu.SMEM((count,), jnp.int32),
        pltpu.SMEM((count,), jnp.int32),
    ] + [pltpu.SMEM((3, count // 2 * (spans * SPAN // (block >> i)) + 8), jnp.int32) for i in range(levels)]


def scratch(spans, count, parts, block=1024, levels=2):
    return [
        pltpu.VMEM((spans // 4 * PIECE, 2 * D), BF16),
        pltpu.VMEM((count * ROWS, D), BF16),
        pltpu.SemaphoreType.DMA((parts,)),
        pltpu.VMEM((8, D), jnp.int32),
        pltpu.SMEM((8, D), jnp.int32),
        pltpu.SemaphoreType.DMA,
    ] + work_shapes(spans, count, block, levels)


def chunk_row(tab, j):
    return pl.ds(pl.multiple_of(jnp.maximum(tab[SLOT, j], 0), 16), SPAN)


def first_kernel(qa_ref, qb_ref, *refs):
    parts, (m_s, acc, page, have), rest = refs[:2], refs[2:6], refs[6:]
    kv_s, q_s, sem, tab_v, tab, tab_sem, *work = rest
    copies = load_parts(parts, kv_s, sem)
    m_s[...] = jnp.full(m_s.shape, LOW, F32)
    acc[...] = jnp.zeros(acc.shape, F32)
    for copy in copies:
        copy.wait()
    tables((0,) * 4 + (1,) * 4, kv_s, (qa_ref, qb_ref), tab_v, tab, tab_sem)
    have[...] = tab_v[SLOT : SLOT + 1, :]
    for j in range(16):
        page[j] = kv_s[chunk_row(tab, j), :]
    place_queries((qa_ref, qb_ref), tab, q_s)
    flash(32, 16, True, tab, q_s, kv_s, m_s, acc, work)


def give_kernel(q_ref, m_in, acc_in, page_in, *refs):
    parts, (give_o, give_p), rest = refs[:4], refs[4:6], refs[6:]
    m_s, acc, levels_s, kv_s, q_s, sem, tab_v, tab, tab_sem, *work = rest
    copies = load_parts(parts, kv_s, sem)
    levels_s[...] = jnp.zeros(levels_s.shape, F32)
    m_s[...] = m_in[8 * ROWS :, :]
    acc[...] = acc_in[8 * ROWS :, :]
    for copy in copies:
        copy.wait()
    tables((0,) * 8 + (1,) * 8, kv_s, (q_ref,), tab_v, tab, tab_sem)
    for j in range(8):
        near = kv_s[chunk_row(tab, j), :].astype(F32)
        give_p[j] = jnp.where(tab[SLOT, j] >= 0, near, page_in[8 + j].astype(F32)).astype(BF16)
    place_queries((q_ref,), tab, q_s)
    flash(64, 8, False, tab, q_s, kv_s, m_s, acc, work)
    for g in range(GROUP):
        for block in range(4):
            logs = []
            for j in (2 * block, 2 * block + 1):
                rows = pl.ds(pl.multiple_of(tab[TURN, j] * ROWS + g * SPAN, SPAN), SPAN)
                sums = jnp.maximum(acc[rows, D:], 1e-30)
                give_o[j * SPAN : (j + 1) * SPAN, g * D : (g + 1) * D] = (acc[rows, :D] * (1.0 / sums)).astype(BF16)
                logs.append(m_s[rows, :] + jnp.log(sums) * math.log2(math.e))
            level = jnp.concatenate(logs, axis=0).T[:1, :]
            for part in range(3):
                piece = level.astype(BF16).astype(F32)
                level = level - piece
                levels_s[part * 4 + g : part * 4 + g + 1, block * D : (block + 1) * D] = piece
    give_o[8 * SPAN :, :] = levels_s[...].astype(BF16)


def own_kernel(q_ref, m_in, acc_in, page_in, have, *refs):
    parts, (m_out, acc_out, page, found), rest = refs[:8], refs[8:12], refs[12:]
    m_s, acc, kv_s, q_s, sem, tab_v, tab, tab_sem, *work = rest
    copies = load_parts(parts, kv_s, sem)
    m_s[...] = m_in[: 8 * ROWS, :]
    acc[...] = acc_in[: 8 * ROWS, :]
    for copy in copies:
        copy.wait()
    tables((0,) * 8 + (1,) * 8 + ((0,) * 4 + (1,) * 4) * 2, kv_s, (q_ref,), tab_v, tab, tab_sem)
    found[...] = jnp.maximum(have[...], tab_v[SLOT : SLOT + 1, :])
    for j in range(8):
        near = kv_s[chunk_row(tab, j), :].astype(F32)
        page[j] = jnp.where(tab[SLOT, j] >= 0, near, page_in[j].astype(F32)).astype(BF16)
    place_queries((q_ref,), tab, q_s)
    flash(128, 8, False, tab, q_s, kv_s, m_s, acc, work)
    for j in range(8):
        rows = pl.ds(pl.multiple_of(tab[TURN, j] * ROWS, ROWS), ROWS)
        m_out[j * ROWS : (j + 1) * ROWS, :] = m_s[rows, :]
        acc_out[j * ROWS : (j + 1) * ROWS, :] = acc[rows, :]


def merge_kernel(m_in, acc_in, take, page, found, take_p, out):
    levels = take[8 * SPAN :, :].astype(F32)
    for g in range(GROUP):
        level = levels[g : g + 1] + levels[4 + g : 5 + g] + levels[8 + g : 9 + g]
        for block in range(4):
            both = jnp.broadcast_to(level[:, block * D : (block + 1) * D], (D, D)).T
            for j in (2 * block, 2 * block + 1):
                y, ab = divmod(j, 2)
                rows = slice(j * ROWS + g * SPAN, j * ROWS + (g + 1) * SPAN)
                m_a, m_b = m_in[rows, :], both[j % 2 * SPAN : (j % 2 + 1) * SPAN]
                top = jnp.maximum(m_a, m_b)
                w_a, w_b = jnp.exp2(m_a - top), jnp.exp2(m_b - top)
                o_b = take[j * SPAN : (j + 1) * SPAN, g * D : (g + 1) * D].astype(F32)
                total = acc_in[rows, D:] * w_a + w_b
                o = (acc_in[rows, :D] * w_a + o_b * w_b) * (1.0 / total)
                out[y, ab * SPAN : (ab + 1) * SPAN, g * D : (g + 1) * D] = o.astype(BF16)
    lane = lax.broadcasted_iota(jnp.int32, (1, D), 1)
    for j in range(8):
        y, s = divmod(j, 2)
        here = jnp.max(jnp.where(lane == j, found[...], -1), axis=1, keepdims=True) >= 0
        x = jnp.where(here, page[j].astype(F32), take_p[j].astype(F32))
        out[y, 2 * SPAN :, s * 2 * D : (s + 1) * 2 * D] = x.astype(BF16)


def finish_kernel(x_ref, o_ref, k_ref, v_ref):
    for h in range(HEADS):
        o_ref[:, h * GROUP * D : (h + 1) * GROUP * D] = x_ref[h, : 2 * SPAN, :]
        for s in range(2):
            at = 2 * s * D
            k_ref[s, :, h * D : (h + 1) * D] = x_ref[h, 2 * SPAN :, at : at + D]
            v_ref[s, :, h * D : (h + 1) * D] = x_ref[h, 2 * SPAN :, at + D : at + 2 * D]


def cost(scores):
    return pl.CostEstimate(flops=scores * 2048, bytes_accessed=2**20, transcendentals=0)


HAVE_SHAPE = jax.ShapeDtypeStruct((1, D), jnp.int32)


def state_shape(count):
    return [jax.ShapeDtypeStruct((count * ROWS, D), F32), jax.ShapeDtypeStruct((count * ROWS, 2 * D), F32)]


STATE = [pltpu.VMEM((8 * ROWS, D), F32), pltpu.VMEM((8 * ROWS, 2 * D), F32)]


def first(q, q_other, parts):
    return pl.pallas_call(
        first_kernel,
        out_shape=(*state_shape(16), jax.ShapeDtypeStruct((16, SPAN, 2 * D), BF16), HAVE_SHAPE),
        in_specs=[VMEM_SPEC] * 2 + [ANY_SPEC] * 2,
        out_specs=(VMEM_SPEC,) * 4,
        scratch_shapes=scratch(32, 16, 2),
        compiler_params=PARAMS,
        cost_estimate=cost(16 * ROWS * 1024),
        name="first",
    )(q, q_other, *parts)


PAGES = jax.ShapeDtypeStruct((8, SPAN, 2 * D), BF16)


def give(q, m, acc, page, parts):
    return pl.pallas_call(
        give_kernel,
        out_shape=(jax.ShapeDtypeStruct((8 * SPAN + META, GROUP * D), BF16), PAGES),
        in_specs=[VMEM_SPEC] * 4 + [ANY_SPEC] * 4,
        out_specs=(VMEM_SPEC,) * 2,
        scratch_shapes=STATE + [pltpu.VMEM((META, GROUP * D), F32)] + scratch(64, 8, 4),
        compiler_params=PARAMS,
        cost_estimate=cost(8 * ROWS * 2048),
        name="give",
    )(q, m, acc, page, *parts)


def own(q, m, acc, page, have, parts):
    return pl.pallas_call(
        own_kernel,
        out_shape=(*state_shape(8), PAGES, HAVE_SHAPE),
        in_specs=[VMEM_SPEC] * 5 + [ANY_SPEC] * 8,
        out_specs=(VMEM_SPEC,) * 4,
        scratch_shapes=STATE + scratch(128, 8, 8),
        compiler_params=PARAMS,
        cost_estimate=cost(8 * ROWS * 4096),
        name="own",
    )(q, m, acc, page, have, *parts)


def merge(m, acc, take, page, found, take_page):
    return pl.pallas_call(
        merge_kernel,
        out_shape=jax.ShapeDtypeStruct((4, 3 * SPAN, GROUP * D), BF16),
        in_specs=[VMEM_SPEC] * 6,
        out_specs=VMEM_SPEC,
        compiler_params=SMALL,
        name="merge",
    )(m, acc, take, page, found, take_page)


def finish(x):
    return pl.pallas_call(
        finish_kernel,
        out_shape=(
            jax.ShapeDtypeStruct((2 * SPAN, HEADS * GROUP * D), BF16),
            jax.ShapeDtypeStruct((2, SPAN, HEADS * D), BF16),
            jax.ShapeDtypeStruct((2, SPAN, HEADS * D), BF16),
        ),
        in_specs=[VMEM_SPEC],
        out_specs=(VMEM_SPEC,) * 3,
        compiler_params=SMALL,
        name="finish",
    )(x)


def local(queries, k, ks, v, vs, span_pos, page_of_slot):
    pack = prep(span_pos, page_of_slot, queries, k, ks, v, vs)
    pack = lax.all_to_all(pack.reshape(HEADS * PACK, 2 * D), "y", 0, 0, tiled=True)
    a, b, q = split(pack.reshape(4, PACK, 2 * D))

    a1, a2, a3 = shift(a, "z", -1), shift(a, "z", 2), shift(a, "z", 1)
    b1, b2, b3 = shift(b, X, -1), shift(b, X, 2), shift(b, X, 1)
    a1, a2, a3, b1, b2, b3, q = lax.optimization_barrier((a1, a2, a3, b1, b2, b3, q))
    q_other = shift(q, "c", 1)
    a, b = join(a, a1, a2, a3, b, b1, b2, b3)
    a_next, a_prev = shift(a, X, -1), shift(a, X, 1)
    b_next, b_prev = shift(b, "z", -1), shift(b, "z", 1)

    m, acc, page, have = first(q, q_other, (a, b))

    near = (a_next, a_prev, b_next, b_prev)
    near, m, acc, page, have = lax.optimization_barrier((near, m, acc, page, have))
    a_next, a_prev, b_next, b_prev = near
    far = (shift(a_prev, X, 1), shift(b_prev, "z", 1), cross(a_next, X, -1), cross(b_next, "z", -1))

    give_o, give_p = give(q_other, m, acc, page, near)
    take, take_page = shift(give_o, "c", 1), shift(give_p, "c", 1)
    m, acc, page, found = own(q, m, acc, page, have, (*near, *far))
    out = merge(m, acc, take, page, found, take_page)
    out = lax.all_to_all(out.reshape(4 * 3 * SPAN, GROUP * D), "y", 0, 0, tiled=True)
    return finish(out.reshape(4, 3 * SPAN, GROUP * D))


def solution(mesh):
    fine = Mesh(mesh.devices.reshape(2, 4, 2, 4, 2), AXES)
    rows, flat = P(AXES, None), P(AXES)
    return jax.shard_map(
        local,
        mesh=fine,
        in_specs=(rows, rows, rows, rows, rows, flat, flat),
        out_specs=(rows, P(AXES, None, None), P(AXES, None, None)),
        check_vma=False,
    )
```

```python
import functools
import math

import jax
import jax.numpy as jnp
from jax import lax
from jax.experimental import pallas as pl
from jax.experimental.pallas import tpu as pltpu
from jax.sharding import Mesh
from jax.sharding import PartitionSpec as P

AXES = ("xh", "z", "c", "y", "xl")
X = ("xh", "xl")
BF16 = jnp.bfloat16
F32 = jnp.float32
SPAN = 64
HEADS = 4
GROUP = 4
D = 128
ROWS = GROUP * SPAN
PAIR = 2 * ROWS
CHUNK = 128
FACTOR = math.log2(math.e) / math.sqrt(D)
LOW = -1e30
META = 16
PIECE = 4 * SPAN + META
PACK = 2 * SPAN + META + 4 * SPAN
RANK, FULL, TURN, SLOT = range(4)
NT = (((1,), (1,)), ((), ()))
VMEM_SPEC = pl.BlockSpec(memory_space=pltpu.VMEM)
SMEM_SPEC = pl.BlockSpec(memory_space=pltpu.SMEM)
ANY_SPEC = pl.BlockSpec(memory_space=pl.ANY)


SMALL = pltpu.CompilerParams(vmem_limit_bytes=8 * 2**20)
PARAMS = pltpu.CompilerParams(vmem_limit_bytes=24 * 2**20)


def shift(x, axis, by):
    size = 2 if axis == "c" else 4
    return lax.ppermute(x, axis, [(i, (i + by) % size) for i in range(size)])


def cross(x, axis, by):
    if axis == "z":
        axes, at = ("z", "c"), lambda i, c: 2 * i + c
    else:
        axes, at = ("xh", "c", "xl"), lambda i, c: i // 2 * 4 + c * 2 + i % 2
    pairs = [(at(i, c), at((i + by) % 4, 1 - c)) for i in range(4) for c in range(2)]
    return lax.ppermute(x, axes, pairs)


def prep_kernel(pos_ref, slot_ref, q_ref, k_ref, ks_ref, v_ref, vs_ref, out):
    rows = k_ref.shape[0]
    row = lax.broadcasted_iota(jnp.int32, (META, 2 * D), 0)
    meta = jnp.zeros((META, 2 * D), F32)
    for r in range(2):
        meta = jnp.where(row == r, pos_ref[r].astype(F32), meta)
        meta = jnp.where(row == 2 + r, slot_ref[r].astype(F32), meta)
    ks, vs = ks_ref[...].astype(F32).T, vs_ref[...].astype(F32).T
    for h in range(HEADS):
        at = slice(h * D, (h + 1) * D)
        out[h, :rows, :D] = (k_ref[:, at].astype(F32) * ks[:, h : h + 1]).astype(BF16)
        out[h, :rows, D:] = (v_ref[:, at].astype(F32) * vs[:, h : h + 1]).astype(BF16)
        out[h, rows : rows + META, :] = meta.astype(BF16)
        for i in range(2):
            first = rows + META + i * rows
            at = slice((h * 2 + i) * 2 * D, (h * 2 + i + 1) * 2 * D)
            out[h, first : first + rows, :] = q_ref[:, at]


def prep(pos, slot, queries, k, ks, v, vs):
    return pl.pallas_call(
        prep_kernel,
        out_shape=jax.ShapeDtypeStruct((HEADS, PACK, 2 * D), BF16),
        in_specs=[SMEM_SPEC] * 2 + [VMEM_SPEC] * 5,
        out_specs=VMEM_SPEC,
        name="prep",
    )(pos, slot, queries, k, ks.T, v, vs.T)


def split_kernel(x_ref, a_ref, b_ref, q_ref):
    note = jnp.concatenate([x_ref[y, 2 * SPAN : 2 * SPAN + META, :].astype(F32)[:4] for y in range(4)], axis=0)
    note = note.astype(BF16)
    for i, ref in enumerate((a_ref, b_ref)):
        for y in range(4):
            ref[y * SPAN : (y + 1) * SPAN, :] = x_ref[y, i * SPAN : (i + 1) * SPAN, :]
        ref[4 * SPAN :, :] = note
    rows = 2 * SPAN
    for y in range(4):
        for i in range(2):
            first = rows + META + i * rows
            q_ref[y * rows : (y + 1) * rows, i * 2 * D : (i + 1) * 2 * D] = x_ref[y, first : first + rows, :]
            q_ref[4 * rows :, i * 2 * D : (i + 1) * 2 * D] = note


def split(x):
    return pl.pallas_call(
        split_kernel,
        out_shape=(
            jax.ShapeDtypeStruct((PIECE, 2 * D), BF16),
            jax.ShapeDtypeStruct((PIECE, 2 * D), BF16),
            jax.ShapeDtypeStruct((8 * SPAN + META, GROUP * D), BF16),
        ),
        in_specs=[VMEM_SPEC],
        out_specs=(VMEM_SPEC,) * 3,
        compiler_params=SMALL,
        name="split",
    )(x)


def join_kernel(*refs):
    for i, ref in enumerate(refs[:8]):
        refs[8 + i // 4][i % 4 * PIECE : (i % 4 + 1) * PIECE, :] = ref[...]


def join(*pieces):
    return pl.pallas_call(
        join_kernel,
        out_shape=(jax.ShapeDtypeStruct((4 * PIECE, 2 * D), BF16),) * 2,
        in_specs=[VMEM_SPEC] * 8,
        out_specs=(VMEM_SPEC,) * 2,
        compiler_params=SMALL,
        name="join",
    )(*pieces)


def offsets(pieces):
    return [p * PIECE + y * SPAN for p in range(pieces) for y in range(4)]


def load_parts(parts, kv_s, sem):
    copies, row = [], 0
    for i, part in enumerate(parts):
        copies.append(pltpu.make_async_copy(part, kv_s.at[pl.ds(row, part.shape[0]), :], sem.at[i]))
        row += part.shape[0]
    for copy in copies:
        copy.start()
    return copies


def tables(kinds, kv_s, q_refs, tab_v, tab, sem):
    count = len(kinds) * 4
    row = lax.broadcasted_iota(jnp.int32, (META, D), 0)
    lane = lax.broadcasted_iota(jnp.int32, (META, D), 1)
    place = jnp.zeros((1, D), F32)
    for p, kind in enumerate(kinds):
        x = kv_s[p * PIECE + 4 * SPAN : (p + 1) * PIECE, :D].astype(F32)
        hit = jnp.logical_and(row == (lane - p * 4) * 4 + kind, jnp.logical_and(lane >= p * 4, lane < p * 4 + 4))
        place = place + jnp.sum(jnp.where(hit, x, 0.0), axis=0, keepdims=True)
    q_place, slot = jnp.zeros((1, D), F32), jnp.zeros((1, D), F32)
    for half, ref in enumerate(q_refs):
        x = ref[8 * SPAN :, :D].astype(F32)
        j = lane - half * 8
        hit = jnp.logical_and(jnp.logical_and(j >= 0, j < 8), row == (j // 2) * 4 + j % 2)
        q_place = q_place + jnp.sum(jnp.where(hit, x, 0.0), axis=0, keepdims=True)
        hit = jnp.logical_and(jnp.logical_and(j >= 0, j < 8), row == (j // 2) * 4 + j % 2 + 2)
        slot = slot + jnp.sum(jnp.where(hit, x, 0.0), axis=0, keepdims=True)
    big_row = lax.broadcasted_iota(jnp.int32, (D, D), 0)
    down = jnp.broadcast_to(place, (D, D)).T
    inside = big_row < count

    def below(x, limit, where):
        return jnp.sum(jnp.where(jnp.logical_and(x < limit, where), 1.0, 0.0), axis=0, keepdims=True).astype(jnp.int32)

    tab_v[RANK : RANK + 1, :] = below(down, place, inside)
    tab_v[FULL : FULL + 1, :] = below(down, q_place, inside)
    q_down = jnp.broadcast_to(q_place, (D, D)).T
    big_lane = lax.broadcasted_iota(jnp.int32, (D, D), 1)
    same = jnp.logical_and(big_row // 8 == big_lane // 8, big_row < 8 * len(q_refs))
    tab_v[TURN : TURN + 1, :] = below(q_down, q_place, same) + lane[:1] // 8 * 8
    at = ((big_row // 4) * PIECE + big_row % 4 * SPAN + 1).astype(F32)
    hit = jnp.logical_and(down == slot, inside)
    tab_v[SLOT : SLOT + 1, :] = jnp.sum(jnp.where(hit, at, 0.0), axis=0, keepdims=True).astype(jnp.int32) - 1
    copy = pltpu.make_async_copy(tab_v, tab, sem)
    copy.start()
    copy.wait()


def place_queries(q_refs, tab, q_s):
    for half, q_ref in enumerate(q_refs):
        for j in range(8):
            first = tab[TURN, half * 8 + j] * ROWS
            for g in range(GROUP):
                at = pl.ds(pl.multiple_of(first + g * SPAN, SPAN), SPAN)
                q_s[at, :] = q_ref[j * SPAN : (j + 1) * SPAN, g * D : (g + 1) * D]


def flash(spans, count, diagonal, tab, q_s, kv_s, m_s, acc, work):
    s_a, s_b, p_a, p_b, al_a, al_b, hot, order, full_s, own_s, *lists = work
    block = s_a.shape[1]
    sizes = [block // SPAN >> i for i in range(len(lists))]
    least = sizes[-1]
    for i, row in enumerate(offsets(spans // 4)):
        order[tab[RANK, i]] = row
    for j in range(count):
        full_s[tab[TURN, j]] = tab[FULL, j]
        own_s[tab[TURN, j]] = 1 if diagonal and j < 8 else 0
    if not diagonal:
        key = lax.broadcasted_iota(jnp.int32, (block, D), 0)
        hot[...] = jnp.where(lax.broadcasted_iota(jnp.int32, (block, D), 1) == key // SPAN, 1.0, 0.0).astype(BF16)

    counts = [jnp.int32(0)] * len(lists)
    for pair in range(count // 2):
        seen = jnp.maximum(full_s[2 * pair] + own_s[2 * pair], full_s[2 * pair + 1] + own_s[2 * pair + 1])
        seen = lax.div(seen + least - 1, least) * least
        at = jnp.int32(0)
        for i, (items, per) in enumerate(zip(lists, sizes)):
            some = lax.div(seen - at, per)

            def put(b, _, items=items, per=per, pair=pair, first=counts[i], at=at):
                items[0, first + b] = pair
                items[1, first + b] = jnp.minimum(at + b * per, spans - per)
                items[2, first + b] = at + b * per
                return 0

            lax.fori_loop(0, some, put, 0)
            counts[i] = counts[i] + some
            at = at + some * per
    for items, n in zip(lists, counts):
        for extra in range(3):
            items[0, n + extra] = 0
            items[1, n + extra] = 0
            items[2, n + extra] = 1 << 20

    def sweep(size, items, total):
        per, cols = size // SPAN, slice(0, size)

        def rows_of(t):
            return pl.ds(pl.multiple_of(items[0, t] * PAIR, PAIR), PAIR)

        def keys_of(t, lanes):
            first = items[1, t]
            return jnp.concatenate(
                [kv_s[pl.ds(pl.multiple_of(order[first + i], 16), SPAN), lanes] for i in range(per)], axis=0
            )

        def scores(t, s):
            q, k = q_s[rows_of(t), :], keys_of(t, slice(0, D))
            if not diagonal:
                lane = lax.broadcasted_iota(jnp.int32, (ROWS, D), 1)
                shut = [
                    jnp.where(lane < full_s[items[0, t] * 2 + i] - items[2, t], 0.0, LOW).astype(BF16)
                    for i in range(2)
                ]
                q = jnp.concatenate([q, jnp.concatenate(shut, axis=0)], axis=1)
                k = jnp.concatenate([k, hot[cols, :]], axis=1)
            s[:, cols] = lax.dot_general(q, k, NT, preferred_element_type=F32)

        def weigh(t, s, p, al):
            first = pl.multiple_of(items[0, t] * PAIR, PAIR)
            token = lax.rem(lax.broadcasted_iota(jnp.int32, (CHUNK, D), 0), SPAN) + 1
            lane = lax.broadcasted_iota(jnp.int32, (CHUNK, D), 1)
            for c in range(PAIR // CHUNK):
                r = slice(c * CHUNK, (c + 1) * CHUNK)
                tiles = [s[r, u * D : (u + 1) * D] for u in range(size // D)]
                if diagonal:
                    which = items[0, t] * 2 + c * CHUNK // ROWS
                    limit = (full_s[which] - items[2, t]) * SPAN + own_s[which] * (token + (c * CHUNK) % SPAN)
                    gap = lane - limit
                    tiles = [jnp.where(gap < -u * D, x, LOW) for u, x in enumerate(tiles)]
                top = functools.reduce(jnp.maximum, tiles)
                top = jnp.broadcast_to(jnp.max(top, axis=1, keepdims=True), (CHUNK, D)) * FACTOR
                at = pl.ds(first + c * CHUNK, CHUNK)
                old = m_s[at, :]
                new = jnp.maximum(old, top)
                m_s[at, :] = new
                al[r, :] = jnp.exp2(old - new)
                for u, x in enumerate(tiles):
                    p[r, u * D : (u + 1) * D] = jnp.exp2(x * FACTOR - new).astype(BF16)

        def gather(t, p, al_ref):
            v = keys_of(t, slice(D, 2 * D))
            v = jnp.concatenate([v, jnp.ones((size, D), BF16)], axis=1)
            o = lax.dot(p[:, cols], v, preferred_element_type=F32)
            al = al_ref[...]
            rows = rows_of(t)
            acc[rows, :] = acc[rows, :] * jnp.concatenate([al, al], axis=1) + o

        scores(0, s_a)

        def body(i, _):
            t = 2 * i
            scores(t + 1, s_b)
            weigh(t, s_a, p_a, al_a)
            gather(t, p_a, al_a)
            scores(t + 2, s_a)
            weigh(t + 1, s_b, p_b, al_b)
            gather(t + 1, p_b, al_b)
            return 0

        lax.fori_loop(0, (total + 1) // 2, body, 0)

    for items, per, n in zip(lists, sizes, counts):
        sweep(per * SPAN, items, n)


def work_shapes(spans, count, block, levels):
    return [
        pltpu.VMEM((PAIR, block), F32),
        pltpu.VMEM((PAIR, block), F32),
        pltpu.VMEM((PAIR, block), BF16),
        pltpu.VMEM((PAIR, block), BF16),
        pltpu.VMEM((PAIR, D), F32),
        pltpu.VMEM((PAIR, D), F32),
        pltpu.VMEM((block, D), BF16),
        pltpu.SMEM((spans + 32,), jnp.int32),
        pltpu.SMEM((count,), jnp.int32),
        pltpu.SMEM((count,), jnp.int32),
    ] + [pltpu.SMEM((3, count // 2 * (spans * SPAN // (block >> i)) + 8), jnp.int32) for i in range(levels)]


def scratch(spans, count, parts, block=1024, levels=2):
    return [
        pltpu.VMEM((spans // 4 * PIECE, 2 * D), BF16),
        pltpu.VMEM((count * ROWS, D), BF16),
        pltpu.SemaphoreType.DMA((parts,)),
        pltpu.VMEM((8, D), jnp.int32),
        pltpu.SMEM((8, D), jnp.int32),
        pltpu.SemaphoreType.DMA,
    ] + work_shapes(spans, count, block, levels)


def chunk_row(tab, j):
    return pl.ds(pl.multiple_of(jnp.maximum(tab[SLOT, j], 0), 16), SPAN)


def first_kernel(qa_ref, qb_ref, *refs):
    parts, (m_s, acc, page, have), rest = refs[:2], refs[2:6], refs[6:]
    kv_s, q_s, sem, tab_v, tab, tab_sem, *work = rest
    copies = load_parts(parts, kv_s, sem)
    m_s[...] = jnp.full(m_s.shape, LOW, F32)
    acc[...] = jnp.zeros(acc.shape, F32)
    for copy in copies:
        copy.wait()
    tables((0,) * 4 + (1,) * 4, kv_s, (qa_ref, qb_ref), tab_v, tab, tab_sem)
    have[...] = tab_v[SLOT : SLOT + 1, :]
    for j in range(16):
        page[j] = kv_s[chunk_row(tab, j), :]
    place_queries((qa_ref, qb_ref), tab, q_s)
    flash(32, 16, True, tab, q_s, kv_s, m_s, acc, work)


def give_kernel(q_ref, m_in, acc_in, page_in, *refs):
    parts, (give_o, give_p), rest = refs[:4], refs[4:6], refs[6:]
    m_s, acc, levels_s, kv_s, q_s, sem, tab_v, tab, tab_sem, *work = rest
    copies = load_parts(parts, kv_s, sem)
    levels_s[...] = jnp.zeros(levels_s.shape, F32)
    m_s[...] = m_in[8 * ROWS :, :]
    acc[...] = acc_in[8 * ROWS :, :]
    for copy in copies:
        copy.wait()
    tables((0,) * 8 + (1,) * 8, kv_s, (q_ref,), tab_v, tab, tab_sem)
    for j in range(8):
        near = kv_s[chunk_row(tab, j), :].astype(F32)
        give_p[j] = jnp.where(tab[SLOT, j] >= 0, near, page_in[8 + j].astype(F32)).astype(BF16)
    place_queries((q_ref,), tab, q_s)
    flash(64, 8, False, tab, q_s, kv_s, m_s, acc, work)
    for g in range(GROUP):
        for block in range(4):
            logs = []
            for j in (2 * block, 2 * block + 1):
                rows = pl.ds(pl.multiple_of(tab[TURN, j] * ROWS + g * SPAN, SPAN), SPAN)
                sums = jnp.maximum(acc[rows, D:], 1e-30)
                give_o[j * SPAN : (j + 1) * SPAN, g * D : (g + 1) * D] = (acc[rows, :D] * (1.0 / sums)).astype(BF16)
                logs.append(m_s[rows, :] + jnp.log(sums) * math.log2(math.e))
            level = jnp.concatenate(logs, axis=0).T[:1, :]
            for part in range(3):
                piece = level.astype(BF16).astype(F32)
                level = level - piece
                levels_s[part * 4 + g : part * 4 + g + 1, block * D : (block + 1) * D] = piece
    give_o[8 * SPAN :, :] = levels_s[...].astype(BF16)


def own_kernel(q_ref, m_in, acc_in, page_in, have, *refs):
    parts, (m_out, acc_out, page, found), rest = refs[:8], refs[8:12], refs[12:]
    m_s, acc, kv_s, q_s, sem, tab_v, tab, tab_sem, *work = rest
    copies = load_parts(parts, kv_s, sem)
    m_s[...] = m_in[: 8 * ROWS, :]
    acc[...] = acc_in[: 8 * ROWS, :]
    for copy in copies:
        copy.wait()
    tables((0,) * 8 + (1,) * 8 + ((0,) * 4 + (1,) * 4) * 2, kv_s, (q_ref,), tab_v, tab, tab_sem)
    found[...] = jnp.maximum(have[...], tab_v[SLOT : SLOT + 1, :])
    for j in range(8):
        near = kv_s[chunk_row(tab, j), :].astype(F32)
        page[j] = jnp.where(tab[SLOT, j] >= 0, near, page_in[j].astype(F32)).astype(BF16)
    place_queries((q_ref,), tab, q_s)
    flash(128, 8, False, tab, q_s, kv_s, m_s, acc, work)
    for j in range(8):
        rows = pl.ds(pl.multiple_of(tab[TURN, j] * ROWS, ROWS), ROWS)
        m_out[j * ROWS : (j + 1) * ROWS, :] = m_s[rows, :]
        acc_out[j * ROWS : (j + 1) * ROWS, :] = acc[rows, :]


def merge_kernel(m_in, acc_in, take, page, found, take_p, out):
    levels = take[8 * SPAN :, :].astype(F32)
    for g in range(GROUP):
        level = levels[g : g + 1] + levels[4 + g : 5 + g] + levels[8 + g : 9 + g]
        for block in range(4):
            both = jnp.broadcast_to(level[:, block * D : (block + 1) * D], (D, D)).T
            for j in (2 * block, 2 * block + 1):
                y, ab = divmod(j, 2)
                rows = slice(j * ROWS + g * SPAN, j * ROWS + (g + 1) * SPAN)
                m_a, m_b = m_in[rows, :], both[j % 2 * SPAN : (j % 2 + 1) * SPAN]
                top = jnp.maximum(m_a, m_b)
                w_a, w_b = jnp.exp2(m_a - top), jnp.exp2(m_b - top)
                o_b = take[j * SPAN : (j + 1) * SPAN, g * D : (g + 1) * D].astype(F32)
                total = acc_in[rows, D:] * w_a + w_b
                o = (acc_in[rows, :D] * w_a + o_b * w_b) * (1.0 / total)
                out[y, ab * SPAN : (ab + 1) * SPAN, g * D : (g + 1) * D] = o.astype(BF16)
    lane = lax.broadcasted_iota(jnp.int32, (1, D), 1)
    for j in range(8):
        y, s = divmod(j, 2)
        here = jnp.max(jnp.where(lane == j, found[...], -1), axis=1, keepdims=True) >= 0
        x = jnp.where(here, page[j].astype(F32), take_p[j].astype(F32))
        out[y, 2 * SPAN :, s * 2 * D : (s + 1) * 2 * D] = x.astype(BF16)


def finish_kernel(x_ref, o_ref, k_ref, v_ref):
    for h in range(HEADS):
        o_ref[:, h * GROUP * D : (h + 1) * GROUP * D] = x_ref[h, : 2 * SPAN, :]
        for s in range(2):
            at = 2 * s * D
            k_ref[s, :, h * D : (h + 1) * D] = x_ref[h, 2 * SPAN :, at : at + D]
            v_ref[s, :, h * D : (h + 1) * D] = x_ref[h, 2 * SPAN :, at + D : at + 2 * D]


def cost(scores):
    return pl.CostEstimate(flops=scores * 2048, bytes_accessed=2**20, transcendentals=0)


HAVE_SHAPE = jax.ShapeDtypeStruct((1, D), jnp.int32)


def state_shape(count):
    return [jax.ShapeDtypeStruct((count * ROWS, D), F32), jax.ShapeDtypeStruct((count * ROWS, 2 * D), F32)]


STATE = [pltpu.VMEM((8 * ROWS, D), F32), pltpu.VMEM((8 * ROWS, 2 * D), F32)]


def first(q, q_other, parts):
    return pl.pallas_call(
        first_kernel,
        out_shape=(*state_shape(16), jax.ShapeDtypeStruct((16, SPAN, 2 * D), BF16), HAVE_SHAPE),
        in_specs=[VMEM_SPEC] * 2 + [ANY_SPEC] * 2,
        out_specs=(VMEM_SPEC,) * 4,
        scratch_shapes=scratch(32, 16, 2),
        compiler_params=PARAMS,
        cost_estimate=cost(16 * ROWS * 1024),
        name="first",
    )(q, q_other, *parts)


PAGES = jax.ShapeDtypeStruct((8, SPAN, 2 * D), BF16)


def give(q, m, acc, page, parts):
    return pl.pallas_call(
        give_kernel,
        out_shape=(jax.ShapeDtypeStruct((8 * SPAN + META, GROUP * D), BF16), PAGES),
        in_specs=[VMEM_SPEC] * 4 + [ANY_SPEC] * 4,
        out_specs=(VMEM_SPEC,) * 2,
        scratch_shapes=STATE + [pltpu.VMEM((META, GROUP * D), F32)] + scratch(64, 8, 4),
        compiler_params=PARAMS,
        cost_estimate=cost(8 * ROWS * 2048),
        name="give",
    )(q, m, acc, page, *parts)


def own(q, m, acc, page, have, parts):
    return pl.pallas_call(
        own_kernel,
        out_shape=(*state_shape(8), PAGES, HAVE_SHAPE),
        in_specs=[VMEM_SPEC] * 5 + [ANY_SPEC] * 8,
        out_specs=(VMEM_SPEC,) * 4,
        scratch_shapes=STATE + scratch(128, 8, 8),
        compiler_params=PARAMS,
        cost_estimate=cost(8 * ROWS * 4096),
        name="own",
    )(q, m, acc, page, have, *parts)


def merge(m, acc, take, page, found, take_page):
    return pl.pallas_call(
        merge_kernel,
        out_shape=jax.ShapeDtypeStruct((4, 3 * SPAN, GROUP * D), BF16),
        in_specs=[VMEM_SPEC] * 6,
        out_specs=VMEM_SPEC,
        compiler_params=SMALL,
        name="merge",
    )(m, acc, take, page, found, take_page)


def finish(x):
    return pl.pallas_call(
        finish_kernel,
        out_shape=(
            jax.ShapeDtypeStruct((2 * SPAN, HEADS * GROUP * D), BF16),
            jax.ShapeDtypeStruct((2, SPAN, HEADS * D), BF16),
            jax.ShapeDtypeStruct((2, SPAN, HEADS * D), BF16),
        ),
        in_specs=[VMEM_SPEC],
        out_specs=(VMEM_SPEC,) * 3,
        compiler_params=SMALL,
        name="finish",
    )(x)


def local(queries, k, ks, v, vs, span_pos, page_of_slot):
    pack = prep(span_pos, page_of_slot, queries, k, ks, v, vs)
    pack = lax.all_to_all(pack.reshape(HEADS * PACK, 2 * D), "y", 0, 0, tiled=True)
    a, b, q = split(pack.reshape(4, PACK, 2 * D))

    a1, a2, a3 = shift(a, "z", -1), shift(a, "z", 2), shift(a, "z", 1)
    b1, b2, b3 = shift(b, X, -1), shift(b, X, 2), shift(b, X, 1)
    a1, a2, a3, b1, b2, b3, q = lax.optimization_barrier((a1, a2, a3, b1, b2, b3, q))
    q_other = shift(q, "c", 1)
    a, b = join(a, a1, a2, a3, b, b1, b2, b3)
    a_next, a_prev = shift(a, X, -1), shift(a, X, 1)
    b_next, b_prev = shift(b, "z", -1), shift(b, "z", 1)

    m, acc, page, have = first(q, q_other, (a, b))

    near = (a_next, a_prev, b_next, b_prev)
    near, m, acc, page, have = lax.optimization_barrier((near, m, acc, page, have))
    a_next, a_prev, b_next, b_prev = near
    far = (shift(a_prev, X, 1), shift(b_prev, "z", 1), cross(a_next, X, -1), cross(b_next, "z", -1))

    give_o, give_p = give(q_other, m, acc, page, near)
    take, take_page = shift(give_o, "c", 1), shift(give_p, "c", 1)
    m, acc, page, found = own(q, m, acc, page, have, (*near, *far))
    out = merge(m, acc, take, page, found, take_page)
    out = lax.all_to_all(out.reshape(4 * 3 * SPAN, GROUP * D), "y", 0, 0, tiled=True)
    return finish(out.reshape(4, 3 * SPAN, GROUP * D))


def solution(mesh):
    fine = Mesh(mesh.devices.reshape(2, 4, 2, 4, 2), AXES)
    rows, flat = P(AXES, None), P(AXES)
    return jax.shard_map(
        local,
        mesh=fine,
        in_specs=(rows, rows, rows, rows, rows, flat, flat),
        out_specs=(rows, P(AXES, None, None), P(AXES, None, None)),
        check_vma=False,
    )
```
